512 devices in a mesh: ctx: 128 (over y, z, x_lo), tp: 4 (over x_hi, core).
Axes of the slice: x: 4 (x_hi: 2, x_lo: 2; x = x_hi * 2 + x_lo), y: 4, z: 16, core: 2. Of those that a mesh axis runs over, the one named last changes fastest.
Arguments:
- streams: bfloat16 [3, 16384, 1024], P(None, 'ctx', 'tp'), may hold values from -6 to 6
- short_taps: float32 [3, 3, 1024], P(None, None, 'tp'), may hold values from -4 to 4
- w_first: float32 [33, 64], replicated, may hold values from -4 to 4
- b_first: float32 [64], replicated, may hold values from -3.140625 to 3.140625
- w_second: float32 [64, 64], replicated, may hold values from -0.75 to 0.75
- b_second: float32 [64], replicated, may hold values from -3.140625 to 3.140625
- w_last: float32 [64, 1024], P(None, 'tp'), may hold values from -0.75 to 0.75
- decay_rate: float32 [1024], P('tp'), may hold values from 1.5258789e-05 to 0.03
- skip_gain: float32 [1024], P('tp'), may hold values from 0.5 to 1.5
- cotangent: bfloat16 [16384, 1024], P('ctx', 'tp'), may hold values from -19 to 19
Outputs:
- output: bfloat16 [16384, 1024], P('ctx', 'tp')
- grad_streams: bfloat16 [3, 16384, 1024], P(None, 'ctx', 'tp')
- grad_taps: float32 [3, 3, 1024], P(None, None, 'tp')
- grad_w_first: float32 [33, 64], replicated
- grad_b_first: float32 [64], replicated
- grad_w_second: float32 [64, 64], replicated
- grad_b_second: float32 [64], replicated
- grad_w_last: float32 [64, 1024], P(None, 'tp')
- grad_rate: float32 [1024], P('tp')
- grad_skip: float32 [1024], P('tp')
The draws below stay inside these ranges and needn't reach their ends.
All inputs are finite; a program needn't handle non-finite values.
Results may differ from the reference program's by a relative error of at most 0.012.
Values may be sent and summed in bfloat16 or wider, within the bound.
No kernel may reach another device: no remote copies, remote signals or barrier semaphores. Data moves between devices by JAX's collectives and lax.ppermute only.
A program may use at most 128 MiB of HBM per device.

```python
import math
import jax
import jax.numpy as jnp
from jax import lax

C = 1024
BANDS = 16
HID = 64
FEAT = 33
SEQ = 16384


def draw_cotangent(key, part):
    key = jax.random.fold_in(key, 7)
    position = jnp.arange(SEQ, dtype=jnp.float32) / SEQ
    rising = jnp.exp(math.log(3.0) * position)[:, None]
    values = jnp.clip(jax.random.normal(key, (SEQ, C), jnp.float32), -6.0, 6.0) * rising
    return values.astype(jnp.bfloat16)


def shard_levels(rng, dims, cuts, least, largest):
    def one(dim, shards_of):
        steps = jax.random.uniform(jax.random.fold_in(jax.random.fold_in(rng, 6), dim), (shards_of,), jnp.float32, least / len(cuts), largest / len(cuts))
        return jnp.repeat(jnp.exp(steps), dims[dim] // shards_of).reshape((-1,) + (1,) * (len(dims) - dim - 1))

    gain = one(*cuts[0])
    for cut in cuts[1:]:
        gain = gain * one(*cut)
    return gain


def noise(key, extent, scale, limit, cuts=(), kind=jnp.bfloat16):
    drawn = scale * jax.random.normal(key, extent, jnp.float32)
    if cuts:
        drawn = drawn * shard_levels(key, extent, cuts, -0.22, 0.18)
    return jnp.clip(drawn, -limit, limit).astype(kind)


def setup_inputs(seed: int = 0) -> dict:
    key_list = jax.random.split(jax.random.key(seed), 11)
    streams = noise(key_list[0], (3, SEQ, C), 1.0, 6.0, ((1, 128), (2, 4)))
    short_taps = noise(key_list[1], (3, 3, C), 0.7, 4.0, ((2, 4),), jnp.float32)
    w_first = noise(key_list[2], (FEAT, HID), 1.0, 4.0, (), jnp.float32)
    b_first = jnp.clip(jax.random.uniform(key_list[3], (HID,), jnp.float32, -3.140625, 3.140625), -3.140625, 3.140625)
    w_second = noise(key_list[4], (HID, HID), HID ** -0.5, 0.75, (), jnp.float32)
    b_second = jnp.clip(jax.random.uniform(key_list[5], (HID,), jnp.float32, -3.140625, 3.140625), -3.140625, 3.140625)
    w_last = noise(key_list[6], (HID, C), HID ** -0.5, 0.75, ((1, 4),), jnp.float32)
    decay_rate = jnp.clip(jnp.exp(math.log(0.03) - 7.583797 * jax.random.uniform(key_list[7], (C,), jnp.float32) ** shard_levels(key_list[7], (C,), ((0, 4),), -0.2, 0.2)), 1.52587890625e-05, 0.03)
    skip_gain = jnp.clip(0.5 + 1.0 * jax.random.uniform(key_list[8], (C,), jnp.float32) ** shard_levels(key_list[8], (C,), ((0, 4),), -0.2, 0.2), 0.5, 1.5)
    cotangent = draw_cotangent(jax.random.fold_in(key_list[10], 71), 0)
    return {"streams": streams, "short_taps": short_taps, "w_first": w_first, "b_first": b_first, "w_second": w_second, "b_second": b_second, "w_last": w_last, "decay_rate": decay_rate, "skip_gain": skip_gain, "cotangent": cotangent}


exact_prec = lax.Precision.HIGHEST

def features_at(positions, seq_len, band_count):
    frequency = jnp.arange(1, band_count + 1, dtype=jnp.int32)
    phases = positions[:, None] * frequency[None, :] % seq_len
    angles = 2.0 * math.pi / seq_len * phases.astype(jnp.float32)
    linear = positions.astype(jnp.float32)[:, None] / seq_len
    return jnp.concatenate([linear, jnp.cos(angles), jnp.sin(angles)], axis=1)

def reference(streams, short_taps, w_first, b_first, w_second, b_second, w_last, decay_rate, skip_gain, cotangent):
    seq_len = SEQ
    signal = streams.astype(jnp.float32)
    padded = jnp.pad(signal, ((0, 0), (2, 0), (0, 0)))
    tap_list = [short_taps[:, offset][:, None, :] for offset in range(3)]
    side = tap_list[0] * padded[:, 2:] + tap_list[1] * padded[:, 1:-1] + tap_list[2] * padded[:, :-2]
    query_side, key_side, value_side = (side[0], side[1], side[2])
    gated = (key_side * value_side).astype(jnp.bfloat16)
    gated_full = gated.astype(jnp.float32)
    positions = jnp.arange(seq_len, dtype=jnp.int32)
    pos_float = positions.astype(jnp.float32)
    feat = features_at(positions, seq_len, BANDS)
    pre_one = jnp.dot(feat, w_first, precision=exact_prec) + b_first[None, :]
    act_one = jnp.sin(pre_one)
    pre_two = jnp.dot(act_one, w_second, precision=exact_prec) + b_second[None, :]
    act_two = jnp.sin(pre_two)
    raw_filter = jnp.dot(act_two, w_last, precision=exact_prec)
    window = jnp.sqrt(2.0 * decay_rate)[None, :] * jnp.exp(-decay_rate[None, :] * pos_float[:, None])
    filt = (raw_filter * window).astype(jnp.bfloat16)
    dft_size = 2 * seq_len
    gated_spec = jnp.fft.rfft(gated_full, n=dft_size, axis=0)
    filt_spec = jnp.fft.rfft(filt.astype(jnp.float32), n=dft_size, axis=0)
    long_conv = jnp.fft.irfft(gated_spec * filt_spec, n=dft_size, axis=0)[:seq_len]
    mixed = (long_conv + skip_gain[None, :] * gated_full).astype(jnp.bfloat16)
    mixed_full = mixed.astype(jnp.float32)
    output = (query_side * mixed_full).astype(jnp.bfloat16)
    grad_out = cotangent.astype(jnp.float32)
    grad_mixed = (grad_out * query_side).astype(jnp.bfloat16)
    grad_mixed_full = grad_mixed.astype(jnp.float32)
    grad_spec = jnp.fft.rfft(grad_mixed_full, n=dft_size, axis=0)
    grad_gated = (jnp.fft.irfft(jnp.conj(filt_spec) * grad_spec, n=dft_size, axis=0)[:seq_len] + skip_gain[None, :] * grad_mixed_full).astype(jnp.bfloat16)
    grad_filt = jnp.fft.irfft(jnp.conj(gated_spec) * grad_spec, n=dft_size, axis=0)[:seq_len].astype(jnp.bfloat16)
    grad_skip = lax.optimization_barrier(jnp.sum(grad_mixed_full * gated_full, axis=0))
    grad_gated_full = grad_gated.astype(jnp.float32)
    grad_side = jnp.stack([grad_out * mixed_full, grad_gated_full * value_side, grad_gated_full * key_side])
    grad_pad = jnp.pad(grad_side, ((0, 0), (0, 2), (0, 0)))
    grad_streams = (tap_list[0] * grad_pad[:, :seq_len] + tap_list[1] * grad_pad[:, 1:seq_len + 1] + tap_list[2] * grad_pad[:, 2:]).astype(jnp.bfloat16)
    grad_taps = jnp.stack([lax.optimization_barrier(jnp.sum(grad_side * padded[:, 2 - offset:2 - offset + seq_len], axis=1)) for offset in range(3)], axis=1)
    grad_filt_full = grad_filt.astype(jnp.float32)
    grad_raw = grad_filt_full * window
    grad_rate = lax.optimization_barrier(jnp.sum(grad_filt_full * raw_filter * window * (0.5 / decay_rate[None, :] - pos_float[:, None]), axis=0))
    grad_w_last = jnp.dot(act_two.T, grad_raw, precision=exact_prec)
    grad_pre_two = jnp.dot(grad_raw, w_last.T, precision=exact_prec) * jnp.cos(pre_two)
    grad_w_second = jnp.dot(act_one.T, grad_pre_two, precision=exact_prec)
    grad_b_second = lax.optimization_barrier(jnp.sum(grad_pre_two, axis=0))
    grad_pre_one = jnp.dot(grad_pre_two, w_second.T, precision=exact_prec) * jnp.cos(pre_one)
    grad_w_first = jnp.dot(feat.T, grad_pre_one, precision=exact_prec)
    grad_b_first = lax.optimization_barrier(jnp.sum(grad_pre_one, axis=0))
    return (output, grad_streams, grad_taps, grad_w_first, grad_b_first, grad_w_second, grad_b_second, grad_w_last, grad_rate, grad_skip)
```

```python
import math

import jax
import jax.numpy as jnp
from jax import lax
from jax.sharding import PartitionSpec as P

exact_prec = lax.Precision.HIGHEST


def passed_along(block, axis, distance):
    devices = range(lax.axis_size(axis))
    route = [(i - distance, i) for i in devices if i - distance in devices]
    return lax.ppermute(block, axis, route)


def features_at(positions, seq_len, band_count):
    frequency = jnp.arange(1, band_count + 1, dtype=jnp.int32)
    phases = frequency[:, None] * positions[None, :] % seq_len
    angles = 2.0 * math.pi / seq_len * phases.astype(jnp.float32)
    linear = positions.astype(jnp.float32)[None, :] / seq_len
    return jnp.concatenate([linear, jnp.cos(angles), jnp.sin(angles)], axis=0)


def filter_forward(
    positions, seq_len, band_count, w_first, b_first, w_second, b_second, w_cols, rates
):
    feat = features_at(positions, seq_len, band_count)
    pre_one = jnp.dot(w_first.T, feat, precision=exact_prec) + b_first[:, None]
    pre_two = jnp.dot(w_second.T, jnp.sin(pre_one), precision=exact_prec) + b_second[:, None]
    raw_filter = jnp.dot(w_cols.T, jnp.sin(pre_two), precision=exact_prec)
    window = jnp.sqrt(2.0 * rates)[:, None] * jnp.exp(
        -rates[:, None] * positions.astype(jnp.float32)[None, :]
    )
    return (feat, pre_one, pre_two, raw_filter, window)


def filter_backward(saved, w_second, w_cols, rates, positions, grad_filt):
    feat, pre_one, pre_two, raw_filter, window = saved
    grad_raw = grad_filt * window
    grad_rate = jnp.sum(
        grad_filt
        * raw_filter
        * window
        * (0.5 / rates[:, None] - positions.astype(jnp.float32)[None, :]),
        axis=1,
    )
    grad_w_last = jnp.dot(jnp.sin(pre_two), grad_raw.T, precision=exact_prec)
    grad_pre_two = jnp.dot(w_cols, grad_raw, precision=exact_prec) * jnp.cos(pre_two)
    grad_w_second = jnp.dot(jnp.sin(pre_one), grad_pre_two.T, precision=exact_prec)
    grad_b_second = jnp.sum(grad_pre_two, axis=1)
    grad_pre_one = jnp.dot(w_second, grad_pre_two, precision=exact_prec) * jnp.cos(pre_one)
    grad_w_first = jnp.dot(feat, grad_pre_one.T, precision=exact_prec)
    grad_b_first = jnp.sum(grad_pre_one, axis=1)
    return (grad_w_last, grad_rate, grad_w_first, grad_b_first, grad_w_second, grad_b_second)


def table_pair(count):
    indices = jnp.arange(count, dtype=jnp.int32)
    angles = (
        2.0 * math.pi / count * (indices[:, None] * indices[None, :] % count).astype(jnp.float32)
    )
    return (jnp.cos(angles), jnp.sin(angles))


def dft_tables(rows_count, cols_count):
    cos_rows, sin_rows = table_pair(rows_count)
    cos_cols, sin_cols = table_pair(cols_count)
    total = rows_count * cols_count
    row_index = jnp.arange(rows_count, dtype=jnp.int32)
    col_index = jnp.arange(cols_count, dtype=jnp.int32)
    angles = (
        2.0
        * math.pi
        / total
        * (row_index[:, None] * col_index[None, :] % total).astype(jnp.float32)
    )
    return (cos_rows, sin_rows, cos_cols, sin_cols, jnp.cos(angles), jnp.sin(angles))


def forward_dft(signal, tables):
    cos_rows, sin_rows, cos_cols, sin_cols, twist_cos, twist_sin = tables
    half_rows = signal.shape[1]
    inner_real = jnp.einsum("kn,cnb->ckb", cos_rows[:, :half_rows], signal, precision=exact_prec)
    inner_imag = -jnp.einsum("kn,cnb->ckb", sin_rows[:, :half_rows], signal, precision=exact_prec)
    turned_real = inner_real * twist_cos + inner_imag * twist_sin
    turned_imag = inner_imag * twist_cos - inner_real * twist_sin
    outer_real = jnp.einsum(
        "ckb,bj->ckj", turned_real, cos_cols, precision=exact_prec
    ) + jnp.einsum("ckb,bj->ckj", turned_imag, sin_cols, precision=exact_prec)
    outer_imag = jnp.einsum(
        "ckb,bj->ckj", turned_imag, cos_cols, precision=exact_prec
    ) - jnp.einsum("ckb,bj->ckj", turned_real, sin_cols, precision=exact_prec)
    return (outer_real, outer_imag)


def inverse_dft(spec_real, spec_imag, half_rows, tables):
    cos_rows, sin_rows, cos_cols, sin_cols, twist_cos, twist_sin = tables
    total = cos_rows.shape[0] * cos_cols.shape[0]
    inner_real = jnp.einsum("ckj,jb->ckb", spec_real, cos_cols, precision=exact_prec) - jnp.einsum(
        "ckj,jb->ckb", spec_imag, sin_cols, precision=exact_prec
    )
    inner_imag = jnp.einsum("ckj,jb->ckb", spec_imag, cos_cols, precision=exact_prec) + jnp.einsum(
        "ckj,jb->ckb", spec_real, sin_cols, precision=exact_prec
    )
    turned_real = inner_real * twist_cos - inner_imag * twist_sin
    turned_imag = inner_imag * twist_cos + inner_real * twist_sin
    result = jnp.einsum(
        "nk,ckb->cnb", cos_rows[:half_rows], turned_real, precision=exact_prec
    ) - jnp.einsum("nk,ckb->cnb", sin_rows[:half_rows], turned_imag, precision=exact_prec)
    return result / total


def times_spec(left, right, conjugate_left):
    left_real, left_imag = left
    right_real, right_imag = right
    if conjugate_left:
        left_imag = -left_imag
    return (
        left_real * right_real - left_imag * right_imag,
        left_real * right_imag + left_imag * right_real,
    )


def backward_spectra(
    owner_grad, gated_spec, filt_spec, own_skip, own_count, ctx_count, tok_rows, tables
):
    seq_len = ctx_count * tok_rows
    grad_spec = forward_dft(owner_grad.reshape(own_count, ctx_count, tok_rows), tables)
    back_gated = times_spec(filt_spec, grad_spec, True)
    owner_grad_gated = (
        inverse_dft(back_gated[0], back_gated[1], ctx_count, tables).reshape(own_count, seq_len)
        + own_skip[:, None] * owner_grad
    ).astype(jnp.bfloat16)
    back_filt = times_spec(gated_spec, grad_spec, True)
    owner_grad_filt = (
        inverse_dft(back_filt[0], back_filt[1], ctx_count, tables)
        .reshape(own_count, seq_len)
        .astype(jnp.bfloat16)
    )
    return (owner_grad_gated, owner_grad_filt)


def as_lanes(block, lanes):
    flat = block.reshape(-1)
    return jnp.pad(flat, (0, -flat.shape[0] % lanes)).reshape(-1, lanes)


def summed_everywhere(per_channel, shared):
    peers = lax.axis_size("ctx")
    own_rows = as_lanes(per_channel, peers)
    all_rows = as_lanes(shared, peers)
    parts = jnp.concatenate([own_rows, all_rows], axis=0).T
    count = parts.shape[1]
    parts = jnp.pad(parts, ((0, 0), (0, -count % 128)))
    received = lax.all_to_all(parts, "ctx", split_axis=0, concat_axis=0, tiled=True)
    total = jnp.sum(received, axis=0)
    total = jnp.where(
        jnp.arange(total.shape[0]) < own_rows.shape[0], total, lax.psum(total, "tp")
    )
    spread = jnp.broadcast_to(total[None], parts.shape)
    gathered = lax.all_to_all(spread, "ctx", split_axis=0, concat_axis=0, tiled=True).T
    own_full = gathered[: own_rows.shape[0]].reshape(-1)[: per_channel.size]
    all_full = gathered[own_rows.shape[0] : count].reshape(-1)[: shared.size]
    return own_full.reshape(per_channel.shape), all_full.reshape(shared.shape)


def on_device(
    streams,
    short_taps,
    w_first,
    b_first,
    w_second,
    b_second,
    w_last,
    decay_rate,
    skip_gain,
    cotangent,
):
    ctx_count = lax.axis_size("ctx")
    ctx_rank = lax.axis_index("ctx")
    tok_rows = streams.shape[1]
    channels = streams.shape[2]
    seq_len = tok_rows * ctx_count
    own_count = channels // ctx_count
    band_count = (w_first.shape[0] - 1) // 2
    row_positions = ctx_rank * tok_rows + jnp.arange(tok_rows, dtype=jnp.int32)
    signal = streams.astype(jnp.float32)
    history = passed_along(streams[:, tok_rows - 2 :, :], "ctx", 1)
    padded = jnp.concatenate([history.astype(jnp.float32), signal], axis=1)
    tap_list = [short_taps[:, offset][:, None, :] for offset in range(3)]
    side = (
        tap_list[0] * padded[:, 2:] + tap_list[1] * padded[:, 1:-1] + tap_list[2] * padded[:, :-2]
    )
    query_side, key_side, value_side = (side[0], side[1], side[2])
    gated = (key_side * value_side).astype(jnp.bfloat16)
    grad_out = cotangent.astype(jnp.float32)
    grad_mixed = (grad_out * query_side).astype(jnp.bfloat16)
    own_skip = lax.dynamic_slice_in_dim(skip_gain, ctx_rank * own_count, own_count, 0)
    saved = filter_forward(
        row_positions, seq_len, band_count, w_first, b_first, w_second, b_second, w_last, decay_rate
    )
    row_filt = (saved[3] * saved[4]).astype(jnp.bfloat16)
    spare = jnp.zeros((ctx_count, 2, tok_rows), jnp.bfloat16)
    outgoing = jnp.concatenate(
        [
            gated.T.reshape(ctx_count, own_count, tok_rows),
            row_filt.reshape(ctx_count, own_count, tok_rows),
            grad_mixed.T.reshape(ctx_count, own_count, tok_rows),
            spare,
        ],
        axis=1,
    )
    incoming = lax.all_to_all(outgoing, "ctx", split_axis=0, concat_axis=0, tiled=True)
    owner_gated, owner_filt, owner_grad = (
        incoming[:, own_count * i : own_count * (i + 1)]
        .swapaxes(0, 1)
        .reshape(own_count, seq_len)
        .astype(jnp.float32)
        for i in range(3)
    )
    tables = dft_tables(2 * ctx_count, tok_rows)
    gated_spec = forward_dft(owner_gated.reshape(own_count, ctx_count, tok_rows), tables)
    filt_spec = forward_dft(
        owner_filt.reshape(own_count, ctx_count, tok_rows), tables
    )
    product = times_spec(gated_spec, filt_spec, False)
    long_conv = inverse_dft(product[0], product[1], ctx_count, tables).reshape(own_count, seq_len)
    owner_mixed = (long_conv + own_skip[:, None] * owner_gated).astype(jnp.bfloat16)
    owner_grad_gated, owner_grad_filt = backward_spectra(
        owner_grad, gated_spec, filt_spec, own_skip, own_count, ctx_count, tok_rows, tables
    )
    returning = jnp.concatenate(
        [
            block.reshape(own_count, ctx_count, tok_rows).swapaxes(0, 1)
            for block in (owner_mixed, owner_grad_gated, owner_grad_filt)
        ]
        + [spare],
        axis=1,
    )
    returned = lax.all_to_all(returning, "ctx", split_axis=0, concat_axis=0, tiled=True)
    mixed, grad_gated, row_grad_filt = (
        returned[:, own_count * i : own_count * (i + 1)].reshape(channels, tok_rows)
        for i in range(3)
    )
    mixed, grad_gated = mixed.T, grad_gated.T
    filter_grads = filter_backward(
        saved, w_second, w_last, decay_rate, row_positions, row_grad_filt.astype(jnp.float32)
    )
    mixed_full = mixed.astype(jnp.float32)
    output = (query_side * mixed_full).astype(jnp.bfloat16)
    grad_skip_part = jnp.sum(grad_mixed.astype(jnp.float32) * gated.astype(jnp.float32), axis=0)
    grad_gated_full = grad_gated.astype(jnp.float32)
    grad_side = jnp.stack(
        [grad_out * mixed_full, grad_gated_full * value_side, grad_gated_full * key_side]
    )
    ahead = passed_along(grad_side[:, :2, :], "ctx", -1)
    grad_pad = jnp.concatenate([grad_side, ahead], axis=1)
    grad_streams = (
        tap_list[0] * grad_pad[:, :tok_rows]
        + tap_list[1] * grad_pad[:, 1 : tok_rows + 1]
        + tap_list[2] * grad_pad[:, 2:]
    ).astype(jnp.bfloat16)
    taps_part = jnp.stack(
        [
            jnp.sum(grad_side * padded[:, 2 - offset : 2 - offset + tok_rows], axis=1)
            for offset in range(3)
        ],
        axis=1,
    )
    last_part, rate_part, first_part, first_bias, second_part, second_bias = filter_grads
    per_channel = jnp.concatenate(
        [taps_part.reshape(9, channels), grad_skip_part[None], rate_part[None], last_part], axis=0
    )
    shared = jnp.concatenate(
        [first_part, first_bias[None], second_part, second_bias[None]], axis=0
    )
    per_channel, shared = summed_everywhere(per_channel, shared)
    grad_taps = per_channel[:9].reshape(3, 3, channels)
    grad_skip, grad_rate, grad_w_last = per_channel[9], per_channel[10], per_channel[11:]
    feat_count = first_part.shape[0]
    hid = second_part.shape[0]
    grad_w_first, grad_b_first = shared[:feat_count], shared[feat_count]
    grad_w_second = shared[feat_count + 1 : feat_count + 1 + hid]
    grad_b_second = shared[feat_count + 1 + hid]
    return (
        output,
        grad_streams,
        grad_taps,
        grad_w_first,
        grad_b_first,
        grad_w_second,
        grad_b_second,
        grad_w_last,
        grad_rate,
        grad_skip,
    )


def solution(mesh):
    return jax.shard_map(
        on_device,
        mesh=mesh,
        in_specs=(
            P(None, "ctx", "tp"),
            P(None, None, "tp"),
            P(),
            P(),
            P(),
            P(),
            P(None, "tp"),
            P("tp"),
            P("tp"),
            P("ctx", "tp"),
        ),
        out_specs=(
            P("ctx", "tp"),
            P(None, "ctx", "tp"),
            P(None, None, "tp"),
            P(),
            P(),
            P(),
            P(),
            P(None, "tp"),
            P("tp"),
            P("tp"),
        ),
        check_vma=False,
    )
```

```python
import math

import jax
import jax.numpy as jnp
import ml_dtypes
import numpy as np
from jax import lax
from jax.experimental import pallas as pl
from jax.experimental.pallas import tpu as pltpu
from jax.sharding import PartitionSpec as P

F32 = jnp.float32
BF16 = jnp.bfloat16
BLK = 128
SIDE = 256
CHUNK = 2048
ONES_ROW = 33
LO_ROW = 36
HI_ROW = 69
VMEM = 56 * 1024 * 1024
NT = (((1,), (1,)), ((), ()))


def split_const(table):
    hi = table.astype(ml_dtypes.bfloat16)
    lo = (table - hi.astype(np.float64)).astype(ml_dtypes.bfloat16)
    return hi, lo


def dft_consts():
    total = SIDE * BLK
    k_row = np.arange(SIDE)[:, None]
    n_row = np.arange(BLK)[None, :]
    angle = 2 * np.pi * ((k_row * n_row) % SIDE) / SIDE
    rows = np.concatenate([np.cos(angle), -np.sin(angle)], axis=0)
    rows_hi, rows_lo = split_const(rows)
    fwd_rows = np.concatenate([rows_hi, rows_lo], axis=1)
    back_hi, back_lo = split_const(rows.T / total)
    idx = np.arange(BLK)
    angle = 2 * np.pi * ((idx[:, None] * idx[None, :]) % BLK) / BLK
    cos, sin = np.cos(angle), np.sin(angle)
    cols = np.concatenate(split_const(np.block([[cos, -sin], [sin, cos]])), axis=0)
    back_cols = np.concatenate(split_const(np.block([[cos, sin], [-sin, cos]])), axis=0)
    angle = 2 * np.pi * ((k_row * n_row) % total) / total
    twist = np.concatenate([np.cos(angle), np.sin(angle)], axis=1).astype(np.float32)
    back_rows = np.concatenate([back_hi, back_lo], axis=0)
    return fwd_rows, cols, twist, back_cols, back_rows


def feature_const(seq_len, bands):
    t = np.arange(seq_len)[None, :]
    k = np.arange(1, bands + 1)[:, None]
    angle = 2 * np.pi * ((k * t) % seq_len) / seq_len
    feat = np.concatenate([t / seq_len, np.cos(angle), np.sin(angle)], axis=0)
    hi, lo = split_const(feat)
    count = feat.shape[0]
    table = np.zeros((BLK, seq_len), ml_dtypes.bfloat16)
    table[:count] = hi
    table[ONES_ROW : ONES_ROW + 2] = 1
    table[LO_ROW : LO_ROW + count] = lo
    table[HI_ROW : HI_ROW + count] = hi
    return table


def fit_sin_cos():
    r = np.linspace(0.0, np.pi / 2 * 1.001, 4001)[1:]
    z = r * r
    s = np.linalg.lstsq(np.stack([z**i for i in range(6)], 1), np.sin(r) / r, rcond=None)[0]
    c = np.linalg.lstsq(np.stack([z**i for i in range(6)], 1), np.cos(r), rcond=None)[0]
    return [float(v) for v in s], [float(v) for v in c]


SIN_C, COS_C = fit_sin_cos()


def sin_cos(x):
    n = jnp.round(x * (1.0 / math.pi))
    r = (x - n * 3.140625) - n * 9.67653589793e-4
    parity = n - 2.0 * jnp.floor(n * 0.5)
    sign = 1.0 - 2.0 * parity
    z = r * r
    s = jnp.full_like(z, SIN_C[5])
    c = jnp.full_like(z, COS_C[5])
    for i in range(4, -1, -1):
        s = s * z + SIN_C[i]
        c = c * z + COS_C[i]
    return s * (r * sign), c * sign


def split(x):
    hi = x.astype(BF16)
    return hi, (x - hi.astype(F32)).astype(BF16)


def dot(a, b):
    return jnp.dot(a, b, preferred_element_type=F32)


def dot_nt(a, b, precision=None):
    return lax.dot_general(a, b, NT, preferred_element_type=F32, precision=precision)


def eye():
    row = lax.broadcasted_iota(jnp.int32, (BLK, BLK), 0)
    col = lax.broadcasted_iota(jnp.int32, (BLK, BLK), 1)
    return jnp.where(row == col, 1.0, 0.0).astype(BF16)


def forward_spectra(signals, fwd_rows, cols, twist):
    count = len(signals)
    xs = jnp.concatenate(signals, axis=1)
    inner = dot(fwd_rows[...], jnp.concatenate([xs, xs], axis=0))
    tc, ts = twist[:, :BLK], twist[:, BLK:]
    parts = []
    for s in range(count):
        re = inner[:SIDE, s * BLK : (s + 1) * BLK]
        im = inner[SIDE:, s * BLK : (s + 1) * BLK]
        parts.append(jnp.concatenate([re * tc + im * ts, im * tc - re * ts], axis=1))
    hi, lo = split(jnp.concatenate(parts, axis=0))
    c_hi, c_lo = cols[:SIDE, :], cols[SIDE:, :]
    spec = dot(hi, c_hi) + dot(lo, c_hi) + dot(hi, c_lo)
    return [spec[s * SIDE : (s + 1) * SIDE] for s in range(count)]


def inverse_spectra(spectra, back_cols, back_rows, twist):
    count = len(spectra)
    hi, lo = split(jnp.concatenate(spectra, axis=0))
    c_hi, c_lo = back_cols[:SIDE, :], back_cols[SIDE:, :]
    inner = dot(hi, c_hi) + dot(lo, c_hi) + dot(hi, c_lo)
    tc, ts = twist[:, :BLK], twist[:, BLK:]
    parts = []
    for s in range(count):
        re = inner[s * SIDE : (s + 1) * SIDE, :BLK]
        im = inner[s * SIDE : (s + 1) * SIDE, BLK:]
        parts.append(jnp.concatenate([re * tc - im * ts, im * tc + re * ts], axis=0))
    hi, lo = split(jnp.concatenate(parts, axis=1))
    r_hi, r_lo = back_rows[:BLK, :], back_rows[BLK:, :]
    out = dot(r_hi, hi) + dot(r_hi, lo) + dot(r_lo, hi)
    return [out[:, s * BLK : (s + 1) * BLK] for s in range(count)]


def times(a, b, conj_a):
    ar, ai = a[:, :BLK], a[:, BLK:]
    br, bi = b[:, :BLK], b[:, BLK:]
    if conj_a:
        return jnp.concatenate([ar * br + ai * bi, ar * bi - ai * br], axis=1)
    return jnp.concatenate([ar * br - ai * bi, ar * bi + ai * br], axis=1)


def places():
    row = lax.broadcasted_iota(jnp.int32, (BLK, BLK), 0)
    col = lax.broadcasted_iota(jnp.int32, (BLK, BLK), 1)
    return row, col


def earlier(x, m):
    row, col = places()
    r = pltpu.roll(x, m, 1)
    return jnp.where(col >= m, r, jnp.where(row >= 1, pltpu.roll(r, 1, 0), 0.0))


def later(x, m):
    row, col = places()
    r = pltpu.roll(x, BLK - m, 1)
    return jnp.where(
        col < BLK - m, r, jnp.where(row < BLK - 1, pltpu.roll(r, BLK - 1, 0), 0.0)
    )


def decay_window(own_ref, h):
    row, col = places()
    t = (row * BLK + col).astype(F32)
    rate = jnp.full((BLK, BLK), own_ref[10, h], F32)
    return jnp.sqrt(2.0 * rate) * jnp.exp(-rate * t), 0.5 / rate - t


def pack_kernel(streams_ref, cot_ref, out_ref):
    ident = eye()
    for i in range(4):
        block = cot_ref[...] if i == 3 else streams_ref[i]
        for h in range(2):
            turned = lax.dot_general(
                block[:, h * BLK : (h + 1) * BLK],
                ident,
                (((0,), (0,)), ((), ())),
                preferred_element_type=F32,
            )
            at = (i * 2 + h) * BLK
            out_ref[:, at : at + BLK] = turned.astype(BF16)


def net_kernel(feat_ref, w1_ref, w2_ref, b2_ref, wl_ref, a1_ref, c1_ref, a2_ref, c2_ref, raw_ref):
    one, cos_one = sin_cos(dot(w1_ref[...], feat_ref[...]))
    a1_ref[...] = one.astype(BF16)
    c1_ref[...] = cos_one.astype(BF16)
    hi, lo = split(one)
    pre_two = dot(w2_ref[...], jnp.concatenate([hi, lo, hi], axis=0)) + b2_ref[...]
    two, cos_two = sin_cos(pre_two)
    a2_ref[...] = two.astype(BF16)
    c2_ref[...] = cos_two.astype(BF16)
    for h in range(2):
        row = jnp.sum(wl_ref[:, h : h + 1] * two, axis=0, keepdims=True)
        for j in range(CHUNK // BLK):
            raw_ref[h, j : j + 1, :] = row[:, j * BLK : (j + 1) * BLK]


def filt_kernel(own_ref, raw_ref, fwd_rows, cols, twist, spec_ref):
    signals = [
        (raw_ref[h] * decay_window(own_ref, h)[0]).astype(BF16) for h in range(2)
    ]
    for h, spec in enumerate(forward_spectra(signals, fwd_rows, cols, twist)):
        spec_ref[h] = spec


def owner_kernel(
    own_ref,
    recv_ref,
    raw_ref,
    spec_ref,
    fwd_rows,
    cols,
    twist,
    back_cols,
    back_rows,
    feat_ref,
    w2_ref,
    wl_ref,
    a1_ref,
    c1_ref,
    a2_ref,
    c2_ref,
    back_ref,
    vec_ref,
    line_ref,
):
    xs, sides, cots, gated, grad_mixed = [], [], [], [], []
    for h in range(2):
        x = [
            recv_ref[:, (i * 2 + h) * BLK : (i * 2 + h + 1) * BLK].astype(F32) for i in range(4)
        ]
        shifted = [[x[i], earlier(x[i], 1), earlier(x[i], 2)] for i in range(3)]
        side = [
            own_ref[i * 3, h] * shifted[i][0]
            + own_ref[i * 3 + 1, h] * shifted[i][1]
            + own_ref[i * 3 + 2, h] * shifted[i][2]
            for i in range(3)
        ]
        xs.append(shifted)
        sides.append(side)
        cots.append(x[3])
        gated.append((side[1] * side[2]).astype(BF16))
        grad_mixed.append((x[3] * side[0]).astype(BF16))
    spec = forward_spectra(gated + grad_mixed, fwd_rows, cols, twist)
    products = (
        [times(spec[h], spec[2 + h], True) for h in range(2)]
        + [times(spec[h], spec_ref[h], False) for h in range(2)]
        + [times(spec_ref[h], spec[2 + h], True) for h in range(2)]
    )
    convs = inverse_spectra(products, back_cols, back_rows, twist)

    sums = []
    line_ref[...] = jnp.zeros_like(line_ref)
    for h in range(2):
        grad_filt = convs[h].astype(BF16).astype(F32)
        window, slope = decay_window(own_ref, h)
        grad_raw = grad_filt * window
        sums.append(jnp.sum(grad_raw * raw_ref[h] * slope, axis=0, keepdims=True))
        for n in range(BLK):
            line_ref[h : h + 1, n * BLK : (n + 1) * BLK] = grad_raw[n : n + 1, :]

    w2_hi, w2_lo = split(w2_ref[...])
    w2_stack = jnp.concatenate([w2_hi, w2_hi, w2_lo], axis=1)
    col0 = wl_ref[:, 0:1]
    col1 = wl_ref[:, 1:2]
    shared = jnp.zeros((112, BLK), F32)
    last = jnp.zeros((16, 64), F32)
    for j in range(line_ref.shape[1] // CHUNK):
        at = slice(j * CHUNK, (j + 1) * CHUNK)
        line = line_ref[:, at]
        grad_two = (col0 * line[0:1] + col1 * line[1:2]) * c2_ref[:, at].astype(F32)
        hi, lo = split(grad_two)
        grad_one = dot(w2_stack, jnp.concatenate([hi, lo, hi], axis=0)) * c1_ref[
            :, at
        ].astype(F32)
        left = jnp.concatenate([a1_ref[:, at], feat_ref[0:48, at]], axis=0)
        right = jnp.concatenate([hi, grad_one.astype(BF16)], axis=0)
        shared = shared + dot_nt(left, right)
        line_hi, line_lo = split(line)
        last = last + dot_nt(jnp.concatenate([line_hi, line_lo], axis=0), a2_ref[:, at])

    last = last[:8] + last[8:]
    count = 33
    biases = shared[64 + ONES_ROW : 64 + ONES_ROW + 1]
    low = jnp.concatenate(
        [
            shared[64 : 64 + count, 64:],
            biases[:, 64:],
            biases[:, :64],
            jnp.zeros((64 - count - 2, 64), F32),
        ],
        axis=0,
    )
    packed = jnp.concatenate([shared[:64, :64], low], axis=1).T
    p_hi, p_lo = split(packed)
    back_ref[:, 8 * BLK : 9 * BLK] = jnp.concatenate([p_hi, p_lo], axis=1)
    back_ref[:, 9 * BLK :] = jnp.zeros((BLK, BLK), BF16)

    for h in range(2):
        gain = own_ref[9, h]
        g = gated[h].astype(F32)
        gm = grad_mixed[h].astype(F32)
        mixed = (convs[2 + h] + gain * g).astype(BF16).astype(F32)
        grad_gated = (convs[4 + h] + gain * gm).astype(BF16).astype(F32)
        side = sides[h]
        grad_side = [cots[h] * mixed, grad_gated * side[2], grad_gated * side[1]]
        back_ref[:, h * BLK : (h + 1) * BLK] = (side[0] * mixed).astype(BF16)
        sums.append(jnp.sum(gm * g, axis=0, keepdims=True))
        for i in range(3):
            grad_stream = own_ref[i * 3, h] * grad_side[i]
            for m in range(1, 3):
                grad_stream = grad_stream + own_ref[i * 3 + m, h] * later(grad_side[i], m)
            at = (2 + i * 2 + h) * BLK
            back_ref[:, at : at + BLK] = grad_stream.astype(BF16)
            for m in range(3):
                sums.append(jnp.sum(grad_side[i] * xs[h][i][m], axis=0, keepdims=True))
    sums = jnp.concatenate(sums + [jnp.zeros((64 - len(sums), BLK), F32)], axis=0)
    totals = dot_nt(jnp.ones((8, BLK), F32), sums, lax.Precision.HIGHEST)
    vec_ref[...] = jnp.concatenate(
        [jnp.zeros((1, 64), F32), last[0:1], last[1:2], totals[0:1]], axis=1
    )


def unpack_kernel(recv_ref, out_ref, grad_ref):
    ident = eye()
    for i in range(4):
        for h in range(2):
            at = (i * 2 + h) * BLK
            turned = lax.dot_general(
                recv_ref[:, at : at + BLK],
                ident,
                (((0,), (0,)), ((), ())),
                preferred_element_type=F32,
            ).astype(BF16)
            if i == 0:
                out_ref[:, h * BLK : (h + 1) * BLK] = turned
            else:
                grad_ref[i - 1, :, h * BLK : (h + 1) * BLK] = turned


def final_kernel(
    all_ref, taps_ref, w1_ref, b1_ref, w2_ref, b2_ref, wl_ref, rate_ref, skip_ref
):
    low = all_ref[:, :BLK].T
    high = all_ref[:, BLK:].T
    shared = low[:64]
    flipped = shared[:, 64:]
    w2_ref[...] = shared[:, :64]
    w1_ref[...] = flipped[:33]
    b1_ref[...] = flipped[33:34]
    b2_ref[...] = flipped[34:35]
    wl_ref[:, :BLK] = low[64:]
    wl_ref[:, BLK:] = high[:64]
    rest = high[64:]
    for h in range(2):
        at = slice(h * BLK, (h + 1) * BLK)
        rate_ref[:, at] = rest[h : h + 1]
        skip_ref[:, at] = rest[2 + 10 * h : 3 + 10 * h]
        taps_ref[:, at] = rest[3 + 10 * h : 12 + 10 * h]


def params(**kwargs):
    return pltpu.CompilerParams(vmem_limit_bytes=VMEM, **kwargs)


def stacked_weights(weights, order):
    hi = lax.reduce_precision(weights, 8, 7)
    lo = weights - hi
    return jnp.concatenate([lo if name == "lo" else hi for name in order], axis=0)


def on_device(
    streams,
    short_taps,
    w_first,
    b_first,
    w_second,
    b_second,
    w_last,
    decay_rate,
    skip_gain,
    cotangent,
):
    peers = lax.axis_size("ctx")
    rank = lax.axis_index("ctx")
    tok = streams.shape[1]
    channels = streams.shape[2]
    seq_len = tok * peers
    count, hid = w_first.shape
    vmem = pl.BlockSpec(memory_space=pltpu.VMEM)
    smem = pl.BlockSpec(memory_space=pltpu.SMEM)
    shape = jax.ShapeDtypeStruct

    outgoing = pl.pallas_call(
        pack_kernel,
        out_shape=shape((peers, 8 * tok), BF16),
        name="pack_rows",
    )(streams, cotangent)
    incoming = lax.all_to_all(
        outgoing.reshape(peers, 8, tok), "ctx", split_axis=0, concat_axis=0, tiled=True
    ).reshape(peers, 8 * tok)

    table = jnp.concatenate(
        [short_taps.reshape(9, channels), skip_gain[None], decay_rate[None], w_last], axis=0
    )
    own = lax.dynamic_index_in_dim(
        table.reshape(11 + hid, 2, peers), rank, axis=2, keepdims=False
    )
    own_wl = own[11:]
    fwd_rows, cols, twist, back_cols, back_rows = (jnp.asarray(c) for c in dft_consts())
    feat = jnp.asarray(feature_const(seq_len, (count - 1) // 2))
    b_hi = lax.reduce_precision(b_first, 8, 7)
    w_hi = lax.reduce_precision(w_first, 8, 7)
    w1 = (
        jnp.concatenate(
            [
                w_hi,
                b_hi[None],
                (b_first - b_hi)[None],
                jnp.zeros((LO_ROW - ONES_ROW - 2, hid), F32),
                w_hi,
                w_first - w_hi,
                jnp.zeros((BLK - HI_ROW - count, hid), F32),
            ],
            axis=0,
        )
        .T.astype(BF16)
    )
    w2_hi = lax.reduce_precision(w_second, 8, 7)
    w2 = jnp.concatenate([w2_hi, w2_hi, w_second - w2_hi], axis=0).T.astype(BF16)

    act = shape((hid, seq_len), BF16)
    act_spec = pl.BlockSpec((hid, CHUNK), lambda j: (0, j))
    whole = lambda *dims: pl.BlockSpec(dims, lambda j: (0,) * len(dims))
    a1, c1, a2, c2, raw = pl.pallas_call(
        net_kernel,
        grid=(seq_len // CHUNK,),
        in_specs=[
            pl.BlockSpec((BLK, CHUNK), lambda j: (0, j)),
            whole(hid, BLK),
            whole(hid, 3 * hid),
            whole(hid, 1),
            whole(hid, 2),
        ],
        out_specs=[
            act_spec,
            act_spec,
            act_spec,
            act_spec,
            pl.BlockSpec((2, CHUNK // BLK, BLK), lambda j: (0, j, 0)),
        ],
        out_shape=[act, act, act, act, shape((2, BLK, BLK), F32)],
        compiler_params=params(dimension_semantics=("arbitrary",)),
        name="filter_net",
    )(feat, w1, w2, b_second[:, None], own_wl)
    filt_spec = pl.pallas_call(
        filt_kernel,
        in_specs=[smem] + [vmem] * 4,
        out_specs=vmem,
        out_shape=shape((2, SIDE, SIDE), F32),
        compiler_params=params(),
        name="filter_spectrum",
    )(own, raw, fwd_rows, cols, twist)

    back, vec = pl.pallas_call(
        owner_kernel,
        in_specs=[smem] + [vmem] * 15,
        out_specs=[vmem, vmem],
        out_shape=[shape((peers, 10 * tok), BF16), shape((1, 2 * BLK), F32)],
        scratch_shapes=[pltpu.VMEM((8, seq_len), F32)],
        compiler_params=params(),
        name="convolve_channels",
    )(
        own,
        incoming,
        raw,
        filt_spec,
        fwd_rows,
        cols,
        twist,
        back_cols,
        back_rows,
        feat,
        w_second,
        own_wl,
        a1,
        c1,
        a2,
        c2,
    )
    returned = lax.all_to_all(
        back.reshape(peers, 2, 5 * tok), "ctx", split_axis=0, concat_axis=0, tiled=True
    ).reshape(peers, 10 * tok)
    halves = jnp.sum(returned[:, 8 * tok : 9 * tok].astype(F32), axis=0)
    mine = lax.psum(halves[:64] + halves[64:], "tp")
    vec = jnp.concatenate([mine[None], vec[:, 64:]], axis=1)
    spread = jnp.broadcast_to(vec, (peers, 2 * BLK))
    gathered = lax.all_to_all(spread, "ctx", split_axis=0, concat_axis=0, tiled=True)
    output, grad_streams = pl.pallas_call(
        unpack_kernel,
        out_shape=[shape((tok, channels), BF16), shape((3, tok, channels), BF16)],
        name="unpack_rows",
    )(returned)
    taps, gw1, gb1, gw2, gb2, gwl, rate, skip = pl.pallas_call(
        final_kernel,
        out_shape=[
            shape((9, channels), F32),
            shape((count, hid), F32),
            shape((1, hid), F32),
            shape((hid, hid), F32),
            shape((1, hid), F32),
            shape((hid, channels), F32),
            shape((1, channels), F32),
            shape((1, channels), F32),
        ],
        name="unpack_sums",
    )(gathered)
    return (
        output,
        grad_streams,
        taps.reshape(3, 3, channels),
        gw1,
        gb1[0],
        gw2,
        gb2[0],
        gwl,
        rate[0],
        skip[0],
    )


def solution(mesh):
    return jax.shard_map(
        on_device,
        mesh=mesh,
        in_specs=(
            P(None, "ctx", "tp"),
            P(None, None, "tp"),
            P(),
            P(),
            P(),
            P(),
            P(None, "tp"),
            P("tp"),
            P("tp"),
            P("ctx", "tp"),
        ),
        out_specs=(
            P("ctx", "tp"),
            P(None, "ctx", "tp"),
            P(None, None, "tp"),
            P(),
            P(),
            P(),
            P(),
            P(None, "tp"),
            P("tp"),
            P("tp"),
        ),
        check_vma=False,
    )
```

```python
import math

import jax
import jax.numpy as jnp
import ml_dtypes
import numpy as np
from jax import lax
from jax.experimental import pallas as pl
from jax.experimental.pallas import tpu as pltpu
from jax.sharding import PartitionSpec as P

F32 = jnp.float32
BF16 = jnp.bfloat16
BLK = 128
SIDE = 256
CHUNK = 2048
ONES_ROW = 33
LO_ROW = 36
HI_ROW = 69
VMEM = 56 * 1024 * 1024
NT = (((1,), (1,)), ((), ()))


def split_const(table):
    hi = table.astype(ml_dtypes.bfloat16)
    lo = (table - hi.astype(np.float64)).astype(ml_dtypes.bfloat16)
    return hi, lo


def dft_consts():
    total = SIDE * BLK
    k_row = np.arange(SIDE)[:, None]
    n_row = np.arange(BLK)[None, :]
    angle = 2 * np.pi * ((k_row * n_row) % SIDE) / SIDE
    rows = np.concatenate([np.cos(angle), -np.sin(angle)], axis=0)
    rows_hi, rows_lo = split_const(rows)
    fwd_rows = np.concatenate([rows_hi, rows_lo], axis=1)
    back_hi, back_lo = split_const(rows.T / total)
    idx = np.arange(BLK)
    angle = 2 * np.pi * ((idx[:, None] * idx[None, :]) % BLK) / BLK
    cos, sin = np.cos(angle), np.sin(angle)
    cols = np.concatenate(split_const(np.block([[cos, -sin], [sin, cos]])), axis=0)
    back_cols = np.concatenate(split_const(np.block([[cos, sin], [-sin, cos]])), axis=0)
    angle = 2 * np.pi * ((k_row * n_row) % total) / total
    twist = np.concatenate([np.cos(angle), np.sin(angle)], axis=1).astype(np.float32)
    back_rows = np.concatenate([back_hi, back_lo], axis=0)
    return fwd_rows, cols, twist, back_cols, back_rows


def feature_const(seq_len, bands):
    t = np.arange(seq_len)[None, :]
    k = np.arange(1, bands + 1)[:, None]
    angle = 2 * np.pi * ((k * t) % seq_len) / seq_len
    feat = np.concatenate([t / seq_len, np.cos(angle), np.sin(angle)], axis=0)
    hi, lo = split_const(feat)
    count = feat.shape[0]
    table = np.zeros((BLK, seq_len), ml_dtypes.bfloat16)
    table[:count] = hi
    table[ONES_ROW : ONES_ROW + 2] = 1
    table[LO_ROW : LO_ROW + count] = lo
    table[HI_ROW : HI_ROW + count] = hi
    return table


def fit_sin_cos():
    r = np.cos(np.linspace(0.0, np.pi / 2, 4001))[:-1]
    powers = np.stack([r ** (2 * i) for i in range(6)], 1)
    s = np.linalg.lstsq(powers * r[:, None], np.sin(np.pi * r), rcond=None)[0]
    c = np.linalg.lstsq(powers, np.cos(np.pi * r), rcond=None)[0]
    return [float(v) for v in s], [float(v) for v in c]


SIN_C, COS_C = fit_sin_cos()


def sin_cos_pi(x):
    r = x - 2.0 * jnp.round(x * 0.5)
    z = r * r
    s = SIN_C[5] * z + SIN_C[4]
    c = COS_C[5] * z + COS_C[4]
    for i in range(3, -1, -1):
        s = s * z + SIN_C[i]
        c = c * z + COS_C[i]
    return s * r, c


def split(x):
    hi = x.astype(BF16)
    return hi, (x - hi.astype(F32)).astype(BF16)


def dot(a, b):
    return jnp.dot(a, b, preferred_element_type=F32)


def dot_nt(a, b, precision=None):
    return lax.dot_general(a, b, NT, preferred_element_type=F32, precision=precision)


def eye():
    row = lax.broadcasted_iota(jnp.int32, (BLK, BLK), 0)
    col = lax.broadcasted_iota(jnp.int32, (BLK, BLK), 1)
    return jnp.where(row == col, 1.0, 0.0).astype(BF16)


def forward_spectra(signals, fwd_rows, cols, twist):
    count = len(signals)
    xs = jnp.concatenate(signals, axis=1)
    inner = dot(fwd_rows[...], jnp.concatenate([xs, xs], axis=0))
    tc, ts = twist[:, :BLK], twist[:, BLK:]
    parts = []
    for s in range(count):
        re = inner[:SIDE, s * BLK : (s + 1) * BLK]
        im = inner[SIDE:, s * BLK : (s + 1) * BLK]
        parts.append(jnp.concatenate([re * tc + im * ts, im * tc - re * ts], axis=1))
    hi, lo = split(jnp.concatenate(parts, axis=0))
    c_hi, c_lo = cols[:SIDE, :], cols[SIDE:, :]
    spec = dot(hi, c_hi) + dot(lo, c_hi) + dot(hi, c_lo)
    return [spec[s * SIDE : (s + 1) * SIDE] for s in range(count)]


def inverse_pairs(pairs, back_cols, back_rows, twist):
    joined = []
    for a, b in pairs:
        joined.append(
            jnp.concatenate([a[:, :BLK] - b[:, BLK:], a[:, BLK:] + b[:, :BLK]], axis=1)
        )
    count = len(pairs)
    hi, lo = split(jnp.concatenate(joined, axis=0))
    c_hi, c_lo = back_cols[:SIDE, :], back_cols[SIDE:, :]
    inner = dot(hi, c_hi) + dot(lo, c_hi) + dot(hi, c_lo)
    tc, ts = twist[:, :BLK], twist[:, BLK:]
    parts = []
    for s in range(count):
        re = inner[s * SIDE : (s + 1) * SIDE, :BLK]
        im = inner[s * SIDE : (s + 1) * SIDE, BLK:]
        tr = re * tc - im * ts
        ti = im * tc + re * ts
        parts.append(jnp.concatenate([tr, ti], axis=0))
        parts.append(jnp.concatenate([ti, -tr], axis=0))
    hi, lo = split(jnp.concatenate(parts, axis=1))
    r_hi, r_lo = back_rows[:BLK, :], back_rows[BLK:, :]
    out = dot(r_hi, hi) + dot(r_hi, lo) + dot(r_lo, hi)
    return [out[:, s * BLK : (s + 1) * BLK] for s in range(2 * count)]


def times(a, b, conj_a):
    ar, ai = a[:, :BLK], a[:, BLK:]
    br, bi = b[:, :BLK], b[:, BLK:]
    if conj_a:
        return jnp.concatenate([ar * br + ai * bi, ar * bi - ai * br], axis=1)
    return jnp.concatenate([ar * br - ai * bi, ar * bi + ai * br], axis=1)


def places():
    row = lax.broadcasted_iota(jnp.int32, (BLK, BLK), 0)
    col = lax.broadcasted_iota(jnp.int32, (BLK, BLK), 1)
    return row, col


def earlier(x, m):
    row, col = places()
    r = pltpu.roll(x, m, 1)
    return jnp.where(col >= m, r, jnp.where(row >= 1, pltpu.roll(r, 1, 0), 0.0))


def later(x, m):
    row, col = places()
    r = pltpu.roll(x, BLK - m, 1)
    return jnp.where(
        col < BLK - m, r, jnp.where(row < BLK - 1, pltpu.roll(r, BLK - 1, 0), 0.0)
    )


def picked(x, rank):
    lane = lax.broadcasted_iota(jnp.int32, x.shape, 1)
    return jnp.sum(jnp.where(lane == rank, x, 0.0), axis=1, keepdims=True)


def half(h):
    return slice(h * BLK, (h + 1) * BLK)


def decay_window(rate_ref, rank, h):
    row, col = places()
    t = (row * BLK + col).astype(F32)
    rate = jnp.broadcast_to(picked(rate_ref[:, half(h)], rank), (BLK, BLK))
    return jnp.sqrt(2.0 * rate) * jnp.exp(-rate * t), 0.5 / rate - t


def turned(block):
    return lax.dot_general(
        block, eye(), (((0,), (0,)), ((), ())), preferred_element_type=F32
    )


def pack_kernel(streams_ref, cot_ref, out_ref, hold_ref):
    for i in range(4):
        block = cot_ref[...] if i == 3 else streams_ref[i]
        for h in range(2):
            hold_ref[:, i * 2 + h, :] = turned(block[:, half(h)])
    out_ref[...] = hold_ref[...].astype(BF16)


def net_kernel(
    rank_ref,
    feat_ref,
    w1_ref,
    b1_ref,
    w2_ref,
    b2_ref,
    wl_ref,
    a1_ref,
    c1_ref,
    a2_ref,
    c2_ref,
    raw_ref,
    w1_hold,
    w2_hold,
    wl_hold,
):
    @pl.when(pl.program_id(0) == 0)
    def _():
        def parts(ref):
            x = ref[...] * (1.0 / math.pi)
            hi = x.astype(BF16).astype(F32)
            return hi, x - hi

        w_hi, w_lo = parts(w1_ref)
        b_hi, b_lo = parts(b1_ref)
        count, hid = w_hi.shape
        gap = jnp.zeros((LO_ROW - ONES_ROW - 2, hid), F32)
        end = jnp.zeros((BLK - HI_ROW - count, hid), F32)
        stack = jnp.concatenate([w_hi, b_hi, b_lo, gap, w_hi, w_lo, end], axis=0)
        w1_hold[...] = stack.T.astype(BF16)
        w_hi, w_lo = parts(w2_ref)
        b_hi, b_lo = parts(b2_ref)
        end = jnp.zeros((14, hid), F32)
        stack = jnp.concatenate([w_hi, w_hi, w_lo, b_hi, b_lo, end], axis=0)
        w2_hold[...] = stack.T.astype(BF16)
        rank = rank_ref[0]
        for h in range(2):
            wl_hold[:, half(h)] = jnp.broadcast_to(
                picked(wl_ref[:, half(h)], rank), (hid, BLK)
            )

    one, cos_one = sin_cos_pi(dot(w1_hold[...], feat_ref[...]))
    a1_ref[...] = one.astype(BF16)
    c1_ref[...] = cos_one.astype(BF16)
    hi, lo = split(one)
    ones = jnp.ones((16, CHUNK), BF16)
    two, cos_two = sin_cos_pi(dot(w2_hold[...], jnp.concatenate([hi, lo, hi, ones], axis=0)))
    a2_ref[...] = two.astype(BF16)
    c2_ref[...] = cos_two.astype(BF16)
    for h in range(2):
        col = wl_hold[:, h * BLK : h * BLK + 1]
        row = jnp.sum(col * two, axis=0, keepdims=True)
        for j in range(CHUNK // BLK):
            raw_ref[h, j : j + 1, :] = row[:, j * BLK : (j + 1) * BLK]


def filt_kernel(rank_ref, rate_ref, raw_ref, fwd_rows, cols, twist, spec_ref):
    signals = [
        (raw_ref[h] * decay_window(rate_ref, rank_ref[0], h)[0]).astype(BF16)
        for h in range(2)
    ]
    for h, spec in enumerate(forward_spectra(signals, fwd_rows, cols, twist)):
        spec_ref[h] = spec


def owner_kernel(
    rank_ref,
    taps_ref,
    skip_ref,
    rate_ref,
    w2_ref,
    wl_ref,
    recv_ref,
    raw_ref,
    spec_ref,
    fwd_rows,
    cols,
    twist,
    back_cols,
    back_rows,
    feat_any,
    a1_any,
    c1_any,
    a2_any,
    c2_any,
    back_ref,
    vec_ref,
    line_ref,
    hold_ref,
    feat_ref,
    a1_ref,
    c1_ref,
    a2_ref,
    c2_ref,
    sems,
):
    moves = [
        pltpu.make_async_copy(src, dst, sems.at[k])
        for k, (src, dst) in enumerate(
            [
                (c2_any, c2_ref),
                (c1_any, c1_ref),
                (a1_any, a1_ref),
                (feat_any.at[pl.ds(0, 48), :], feat_ref),
                (a2_any, a2_ref),
            ]
        )
    ]
    for move in moves:
        move.start()
    rank = rank_ref[0]
    hold_ref[...] = recv_ref[...].astype(F32)
    taps, gains = [], []
    xs, sides, cots, gated, grad_mixed = [], [], [], [], []
    for h in range(2):
        gains.append(picked(skip_ref[:, half(h)], rank))
        taps.append([])
        for i in range(3):
            own = picked(taps_ref[i, :, half(h)], rank)
            taps[h].append([own[m : m + 1] for m in range(3)])
        x = [hold_ref[:, i * 2 + h, :] for i in range(4)]
        shifted = [[x[i], earlier(x[i], 1), earlier(x[i], 2)] for i in range(3)]
        side = [
            taps[h][i][0] * shifted[i][0]
            + taps[h][i][1] * shifted[i][1]
            + taps[h][i][2] * shifted[i][2]
            for i in range(3)
        ]
        xs.append(shifted)
        sides.append(side)
        cots.append(x[3])
        gated.append((side[1] * side[2]).astype(BF16))
        grad_mixed.append((x[3] * side[0]).astype(BF16))
    spec = forward_spectra(gated + grad_mixed, fwd_rows, cols, twist)
    pairs = [
        [times(spec[h], spec[2 + h], True) for h in range(2)],
        [times(spec[h], spec_ref[h], False) for h in range(2)],
        [times(spec_ref[h], spec[2 + h], True) for h in range(2)],
    ]
    convs = inverse_pairs(pairs, back_cols, back_rows, twist)

    sums = []
    line_ref[...] = jnp.zeros_like(line_ref)
    for h in range(2):
        grad_filt = convs[h].astype(BF16).astype(F32)
        window, slope = decay_window(rate_ref, rank, h)
        grad_raw = grad_filt * window
        sums.append(jnp.sum(grad_raw * raw_ref[h] * slope, axis=0, keepdims=True))
        for n in range(BLK):
            line_ref[h : h + 1, n * BLK : (n + 1) * BLK] = grad_raw[n : n + 1, :]

    w2_hi, w2_lo = split(w2_ref[...])
    w2_stack = jnp.concatenate([w2_hi, w2_hi, w2_lo], axis=1)
    col0 = picked(wl_ref[:, half(0)], rank)
    col1 = picked(wl_ref[:, half(1)], rank)
    total = jnp.zeros((BLK, 192), F32)
    for move in moves:
        move.wait()
    for j in range(line_ref.shape[1] // CHUNK):
        at = slice(j * CHUNK, (j + 1) * CHUNK)
        line = line_ref[:, at]
        grad_two = (col0 * line[0:1] + col1 * line[1:2]) * c2_ref[:, at].astype(F32)
        hi, lo = split(grad_two)
        grad_one = dot(w2_stack, jnp.concatenate([hi, lo, hi], axis=0)) * c1_ref[
            :, at
        ].astype(F32)
        line_hi = line.astype(BF16).astype(F32)
        lines = jnp.concatenate([line_hi, line - line_hi], axis=0).astype(BF16)
        left = jnp.concatenate([a1_ref[:, at], feat_ref[:, at], lines], axis=0)
        right = jnp.concatenate([hi, grad_one.astype(BF16), a2_ref[:, at]], axis=0)
        total = total + dot_nt(left, right)

    shared = total[:112, :BLK]
    last = total[112:120, BLK:] + total[120:, BLK:]
    count = 33
    biases = shared[64 + ONES_ROW : 64 + ONES_ROW + 1]
    low = jnp.concatenate(
        [
            shared[64 : 64 + count, 64:],
            biases[:, 64:],
            biases[:, :64],
            jnp.zeros((64 - count - 2, 64), F32),
        ],
        axis=0,
    )
    packed = jnp.concatenate([shared[:64, :64], low], axis=1).T
    p_hi, p_lo = split(packed)
    back_ref[:, 8 * BLK : 9 * BLK] = jnp.concatenate([p_hi, p_lo], axis=1)
    back_ref[:, 9 * BLK :] = jnp.zeros((BLK, BLK), BF16)

    for h in range(2):
        g = gated[h].astype(F32)
        gm = grad_mixed[h].astype(F32)
        mixed = (convs[2 + h] + gains[h] * g).astype(BF16).astype(F32)
        grad_gated = (convs[4 + h] + gains[h] * gm).astype(BF16).astype(F32)
        side = sides[h]
        grad_side = [cots[h] * mixed, grad_gated * side[2], grad_gated * side[1]]
        back_ref[:, h * BLK : (h + 1) * BLK] = (side[0] * mixed).astype(BF16)
        sums.append(jnp.sum(gm * g, axis=0, keepdims=True))
        for i in range(3):
            grad_stream = taps[h][i][0] * grad_side[i]
            for m in range(1, 3):
                grad_stream = grad_stream + taps[h][i][m] * later(grad_side[i], m)
            at = (2 + i * 2 + h) * BLK
            back_ref[:, at : at + BLK] = grad_stream.astype(BF16)
            for m in range(3):
                sums.append(jnp.sum(grad_side[i] * xs[h][i][m], axis=0, keepdims=True))
    sums = jnp.concatenate(sums + [jnp.zeros((64 - len(sums), BLK), F32)], axis=0)
    totals = dot_nt(jnp.ones((8, BLK), F32), sums, lax.Precision.HIGHEST)
    vec_ref[...] = jnp.concatenate(
        [jnp.zeros((1, 64), F32), last[0:1], last[1:2], totals[0:1]], axis=1
    )


def unpack_kernel(recv_ref, out_ref, grad_ref):
    for i in range(4):
        for h in range(2):
            at = (i * 2 + h) * BLK
            block = turned(recv_ref[:, at : at + BLK]).astype(BF16)
            if i == 0:
                out_ref[:, half(h)] = block
            else:
                grad_ref[i - 1, :, half(h)] = block


def final_kernel(
    all_ref, taps_ref, w1_ref, b1_ref, w2_ref, b2_ref, wl_ref, rate_ref, skip_ref
):
    low = all_ref[:, :BLK].T
    high = all_ref[:, BLK:].T
    shared = low[:64]
    flipped = shared[:, 64:]
    w2_ref[...] = shared[:, :64]
    w1_ref[...] = flipped[:33]
    b1_ref[...] = flipped[33:34]
    b2_ref[...] = flipped[34:35]
    wl_ref[:, :BLK] = low[64:]
    wl_ref[:, BLK:] = high[:64]
    rest = high[64:]
    for h in range(2):
        rate_ref[:, half(h)] = rest[h : h + 1]
        skip_ref[:, half(h)] = rest[2 + 10 * h : 3 + 10 * h]
        for i in range(3):
            at = 3 + 10 * h + 3 * i
            taps_ref[i, :, half(h)] = rest[at : at + 3]


def params(**kwargs):
    return pltpu.CompilerParams(vmem_limit_bytes=VMEM, **kwargs)


def on_device(
    streams,
    short_taps,
    w_first,
    b_first,
    w_second,
    b_second,
    w_last,
    decay_rate,
    skip_gain,
    cotangent,
):
    peers = lax.axis_size("ctx")
    rank = lax.axis_index("ctx")
    tok = streams.shape[1]
    channels = streams.shape[2]
    seq_len = tok * peers
    count, hid = w_first.shape
    vmem = pl.BlockSpec(memory_space=pltpu.VMEM)
    smem = pl.BlockSpec(memory_space=pltpu.SMEM)
    shape = jax.ShapeDtypeStruct

    row = rank.reshape(1).astype(jnp.int32)
    outgoing = pl.pallas_call(
        pack_kernel,
        out_shape=shape((peers, 8, tok), BF16),
        scratch_shapes=[pltpu.VMEM((peers, 8, tok), F32)],
        name="pack_rows",
    )(streams, cotangent)
    incoming = lax.all_to_all(outgoing, "ctx", split_axis=0, concat_axis=0, tiled=True)

    fwd_rows, cols, twist, back_cols, back_rows = (jnp.asarray(c) for c in dft_consts())
    feat = jnp.asarray(feature_const(seq_len, (count - 1) // 2))
    act = shape((hid, seq_len), BF16)
    act_spec = pl.BlockSpec((hid, CHUNK), lambda j: (0, j))
    whole = lambda *dims: pl.BlockSpec(dims, lambda j: (0,) * len(dims))
    a1, c1, a2, c2, raw = pl.pallas_call(
        net_kernel,
        grid=(seq_len // CHUNK,),
        in_specs=[
            smem,
            pl.BlockSpec((BLK, CHUNK), lambda j: (0, j)),
            whole(count, hid),
            whole(1, hid),
            whole(hid, hid),
            whole(1, hid),
            whole(hid, channels),
        ],
        out_specs=[
            act_spec,
            act_spec,
            act_spec,
            act_spec,
            pl.BlockSpec((2, CHUNK // BLK, BLK), lambda j: (0, j, 0)),
        ],
        out_shape=[act, act, act, act, shape((2, BLK, BLK), F32)],
        scratch_shapes=[
            pltpu.VMEM((hid, BLK), BF16),
            pltpu.VMEM((hid, 3 * hid + 16), BF16),
            pltpu.VMEM((hid, 2 * BLK), F32),
        ],
        compiler_params=params(dimension_semantics=("arbitrary",)),
        name="filter_net",
    )(row, feat, w_first, b_first[None], w_second, b_second[None], w_last)
    filt_spec = pl.pallas_call(
        filt_kernel,
        in_specs=[smem] + [vmem] * 5,
        out_specs=vmem,
        out_shape=shape((2, SIDE, SIDE), F32),
        compiler_params=params(),
        name="filter_spectrum",
    )(row, decay_rate[None], raw, fwd_rows, cols, twist)

    back, vec = pl.pallas_call(
        owner_kernel,
        in_specs=[smem] + [vmem] * 13 + [pl.BlockSpec(memory_space=pl.ANY)] * 5,
        out_specs=[vmem, vmem],
        out_shape=[shape((peers, 10 * tok), BF16), shape((1, 2 * BLK), F32)],
        scratch_shapes=[
            pltpu.VMEM((8, seq_len), F32),
            pltpu.VMEM((peers, 8, tok), F32),
            pltpu.VMEM((48, seq_len), BF16),
            pltpu.VMEM((hid, seq_len), BF16),
            pltpu.VMEM((hid, seq_len), BF16),
            pltpu.VMEM((hid, seq_len), BF16),
            pltpu.VMEM((hid, seq_len), BF16),
            pltpu.SemaphoreType.DMA((5,)),
        ],
        compiler_params=params(),
        name="convolve_channels",
    )(
        row,
        short_taps,
        skip_gain[None],
        decay_rate[None],
        w_second,
        w_last,
        incoming,
        raw,
        filt_spec,
        fwd_rows,
        cols,
        twist,
        back_cols,
        back_rows,
        feat,
        a1,
        c1,
        a2,
        c2,
    )
    returned = lax.all_to_all(
        back.reshape(peers, 2, 5 * tok), "ctx", split_axis=0, concat_axis=0, tiled=True
    ).reshape(peers, 10 * tok)
    returned, vec = lax.optimization_barrier((returned, vec))
    halves = jnp.sum(returned[:, 8 * tok : 9 * tok].astype(F32), axis=0)
    mine = lax.psum(halves[:64] + halves[64:], "tp")
    vec = jnp.concatenate([mine[None], vec[:, 64:]], axis=1)
    spread = jnp.broadcast_to(vec, (peers, 2 * BLK))
    gathered = lax.all_to_all(spread, "ctx", split_axis=0, concat_axis=0, tiled=True)
    output, grad_streams = pl.pallas_call(
        unpack_kernel,
        out_shape=[shape((tok, channels), BF16), shape((3, tok, channels), BF16)],
        name="unpack_rows",
    )(returned)
    taps, gw1, gb1, gw2, gb2, gwl, rate, skip = pl.pallas_call(
        final_kernel,
        out_shape=[
            shape((3, 3, channels), F32),
            shape((count, hid), F32),
            shape((1, hid), F32),
            shape((hid, hid), F32),
            shape((1, hid), F32),
            shape((hid, channels), F32),
            shape((1, channels), F32),
            shape((1, channels), F32),
        ],
        name="unpack_sums",
    )(gathered)
    return (
        output,
        grad_streams,
        taps,
        gw1,
        gb1[0],
        gw2,
        gb2[0],
        gwl,
        rate[0],
        skip[0],
    )


def solution(mesh):
    return jax.shard_map(
        on_device,
        mesh=mesh,
        in_specs=(
            P(None, "ctx", "tp"),
            P(None, None, "tp"),
            P(),
            P(),
            P(),
            P(),
            P(None, "tp"),
            P("tp"),
            P("tp"),
            P("ctx", "tp"),
        ),
        out_specs=(
            P("ctx", "tp"),
            P(None, "ctx", "tp"),
            P(None, None, "tp"),
            P(),
            P(),
            P(),
            P(),
            P(None, "tp"),
            P("tp"),
            P("tp"),
        ),
        check_vma=False,
    )
```

```python
import math

import jax
import jax.numpy as jnp
import ml_dtypes
import numpy as np
from jax import lax
from jax.experimental import pallas as pl
from jax.experimental.pallas import tpu as pltpu
from jax.sharding import PartitionSpec as P

F32 = jnp.float32
BF16 = jnp.bfloat16
BLK = 128
SIDE = 256
CHUNK = 2048
ONES_ROW = 33
LO_ROW = 36
HI_ROW = 69
AHEAD_HI = 16
AHEAD_LO = 32
VMEM = 56 * 1024 * 1024
NT = (((1,), (1,)), ((), ()))


def split_const(table):
    hi = table.astype(ml_dtypes.bfloat16)
    lo = (table - hi.astype(np.float64)).astype(ml_dtypes.bfloat16)
    return hi, lo


def dft_consts():
    total = SIDE * BLK
    k_row = np.arange(SIDE)[:, None]
    n_row = np.arange(BLK)[None, :]
    angle = 2 * np.pi * ((k_row * n_row) % SIDE) / SIDE
    rows = np.concatenate([np.cos(angle), -np.sin(angle)], axis=0)
    rows_hi, rows_lo = split_const(rows)
    fwd_rows = np.concatenate([rows_hi, rows_lo], axis=1)
    back_hi, back_lo = split_const(rows.T / total)
    idx = np.arange(BLK)
    angle = 2 * np.pi * ((idx[:, None] * idx[None, :]) % BLK) / BLK
    cos, sin = np.cos(angle), np.sin(angle)
    cols = np.concatenate(split_const(np.block([[cos, -sin], [sin, cos]])), axis=0)
    back_cols = np.concatenate(split_const(np.block([[cos, sin], [-sin, cos]])), axis=0)
    angle = 2 * np.pi * ((k_row * n_row) % total) / total
    twist = np.concatenate([np.cos(angle), np.sin(angle)], axis=1).astype(np.float32)
    back_rows = np.concatenate([back_hi, back_lo], axis=0)
    return fwd_rows, cols, twist, back_cols, back_rows


def feature_const(seq_len, bands):
    t = np.arange(seq_len)[None, :]
    k = np.arange(1, bands + 1)[:, None]
    angle = 2 * np.pi * ((k * t) % seq_len) / seq_len
    feat = np.concatenate([t / seq_len, np.cos(angle), np.sin(angle)], axis=0)
    hi, lo = split_const(feat)
    count = feat.shape[0]
    table = np.zeros((BLK, seq_len), ml_dtypes.bfloat16)
    table[:count] = hi
    table[ONES_ROW : ONES_ROW + 2] = 1
    table[LO_ROW : LO_ROW + count] = lo
    table[HI_ROW : HI_ROW + count] = hi
    return table


def fit_sin_cos():
    r = np.cos(np.linspace(0.0, np.pi / 2, 4001))[:-1]
    powers = np.stack([r ** (2 * i) for i in range(6)], 1)
    s = np.linalg.lstsq(powers * r[:, None], np.sin(np.pi * r), rcond=None)[0]
    c = np.linalg.lstsq(powers, np.cos(np.pi * r), rcond=None)[0]
    return [float(v) for v in s], [float(v) for v in c]


SIN_C, COS_C = fit_sin_cos()


def sin_cos_pi(x):
    r = x - 2.0 * jnp.round(x * 0.5)
    z = r * r
    s = SIN_C[5] * z + SIN_C[4]
    c = COS_C[5] * z + COS_C[4]
    for i in range(3, -1, -1):
        s = s * z + SIN_C[i]
        c = c * z + COS_C[i]
    return s * r, c


def split(x):
    hi = x.astype(BF16)
    return hi, (x - hi.astype(F32)).astype(BF16)


def dot(a, b):
    return jnp.dot(a, b, preferred_element_type=F32)


def dot_nt(a, b, precision=None):
    return lax.dot_general(a, b, NT, preferred_element_type=F32, precision=precision)


def eye():
    row = lax.broadcasted_iota(jnp.int32, (BLK, BLK), 0)
    col = lax.broadcasted_iota(jnp.int32, (BLK, BLK), 1)
    return jnp.where(row == col, 1.0, 0.0).astype(BF16)


def forward_spectra(signals, fwd_rows, cols, twist):
    count = len(signals)
    xs = jnp.concatenate(signals, axis=1)
    inner = dot(fwd_rows[...], jnp.concatenate([xs, xs], axis=0))
    tc, ts = twist[:, :BLK], twist[:, BLK:]
    parts = []
    for s in range(count):
        re = inner[:SIDE, s * BLK : (s + 1) * BLK]
        im = inner[SIDE:, s * BLK : (s + 1) * BLK]
        parts.append(jnp.concatenate([re * tc + im * ts, im * tc - re * ts], axis=1))
    hi, lo = split(jnp.concatenate(parts, axis=0))
    c_hi, c_lo = cols[:SIDE, :], cols[SIDE:, :]
    spec = dot(hi, c_hi) + dot(lo, c_hi) + dot(hi, c_lo)
    return [spec[s * SIDE : (s + 1) * SIDE] for s in range(count)]


def inverse_pairs(pairs, back_cols, back_rows, twist):
    joined = []
    for a, b in pairs:
        joined.append(
            jnp.concatenate([a[:, :BLK] - b[:, BLK:], a[:, BLK:] + b[:, :BLK]], axis=1)
        )
    count = len(pairs)
    hi, lo = split(jnp.concatenate(joined, axis=0))
    c_hi, c_lo = back_cols[:SIDE, :], back_cols[SIDE:, :]
    inner = dot(hi, c_hi) + dot(lo, c_hi) + dot(hi, c_lo)
    tc, ts = twist[:, :BLK], twist[:, BLK:]
    parts = []
    for s in range(count):
        re = inner[s * SIDE : (s + 1) * SIDE, :BLK]
        im = inner[s * SIDE : (s + 1) * SIDE, BLK:]
        tr = re * tc - im * ts
        ti = im * tc + re * ts
        parts.append(jnp.concatenate([tr, ti], axis=0))
        parts.append(jnp.concatenate([ti, -tr], axis=0))
    hi, lo = split(jnp.concatenate(parts, axis=1))
    r_hi, r_lo = back_rows[:BLK, :], back_rows[BLK:, :]
    out = dot(r_hi, hi) + dot(r_hi, lo) + dot(r_lo, hi)
    return [out[:, s * BLK : (s + 1) * BLK] for s in range(2 * count)]


def times(a, b, conj_a):
    ar, ai = a[:, :BLK], a[:, BLK:]
    br, bi = b[:, :BLK], b[:, BLK:]
    if conj_a:
        return jnp.concatenate([ar * br + ai * bi, ar * bi - ai * br], axis=1)
    return jnp.concatenate([ar * br - ai * bi, ar * bi + ai * br], axis=1)


def places():
    row = lax.broadcasted_iota(jnp.int32, (BLK, BLK), 0)
    col = lax.broadcasted_iota(jnp.int32, (BLK, BLK), 1)
    return row, col


def earlier(x, m):
    row, col = places()
    r = pltpu.roll(x, m, 1)
    return jnp.where(col >= m, r, jnp.where(row >= 1, pltpu.roll(r, 1, 0), 0.0))


def later(x, m):
    row, col = places()
    r = pltpu.roll(x, BLK - m, 1)
    return jnp.where(
        col < BLK - m, r, jnp.where(row < BLK - 1, pltpu.roll(r, BLK - 1, 0), 0.0)
    )


def picked(x, rank):
    lane = lax.broadcasted_iota(jnp.int32, x.shape, 1)
    return jnp.sum(jnp.where(lane == rank, x, 0.0), axis=1, keepdims=True)


def half(h):
    return slice(h * BLK, (h + 1) * BLK)


def decay_window(rate_ref, rank, h):
    row, col = places()
    t = (row * BLK + col).astype(F32)
    rate = jnp.broadcast_to(picked(rate_ref[:, half(h)], rank), (BLK, BLK))
    return jnp.sqrt(2.0 * rate) * jnp.exp(-rate * t), 0.5 / rate - t


def turned(block):
    return lax.dot_general(
        block, eye(), (((0,), (0,)), ((), ())), preferred_element_type=F32
    )


def pack_kernel(streams_ref, cot_ref, out_ref, hold_ref):
    for i in range(4):
        block = cot_ref[...] if i == 3 else streams_ref[i]
        for h in range(2):
            hold_ref[:, i * 2 + h, :] = turned(block[:, half(h)])
    out_ref[...] = hold_ref[...].astype(BF16)


def net_kernel(
    rank_ref,
    feat_ref,
    w1_ref,
    b1_ref,
    w2_ref,
    b2_ref,
    wl_ref,
    a1_ref,
    c1_ref,
    a2_ref,
    c2_ref,
    raw_ref,
    w1_hold,
    w2_hold,
    wl_hold,
):
    @pl.when(pl.program_id(0) == 0)
    def _():
        def parts(ref):
            x = ref[...] * (1.0 / math.pi)
            hi = x.astype(BF16).astype(F32)
            return hi, x - hi

        w_hi, w_lo = parts(w1_ref)
        b_hi, b_lo = parts(b1_ref)
        count, hid = w_hi.shape
        gap = jnp.zeros((LO_ROW - ONES_ROW - 2, hid), F32)
        end = jnp.zeros((BLK - HI_ROW - count, hid), F32)
        stack = jnp.concatenate([w_hi, b_hi, b_lo, gap, w_hi, w_lo, end], axis=0)
        w1_hold[...] = stack.T.astype(BF16)
        w_hi, w_lo = parts(w2_ref)
        b_hi, b_lo = parts(b2_ref)
        end = jnp.zeros((14, hid), F32)
        stack = jnp.concatenate([w_hi, w_hi, w_lo, b_hi, b_lo, end], axis=0)
        w2_hold[...] = stack.T.astype(BF16)
        rank = rank_ref[0]
        for h in range(2):
            wl_hold[:, half(h)] = jnp.broadcast_to(
                picked(wl_ref[:, half(h)], rank), (hid, BLK)
            )

    one, cos_one = sin_cos_pi(dot(w1_hold[...], feat_ref[...]))
    a1_ref[...] = one.astype(BF16)
    c1_ref[...] = cos_one.astype(BF16)
    hi, lo = split(one)
    ones = jnp.ones((16, CHUNK), BF16)
    two, cos_two = sin_cos_pi(dot(w2_hold[...], jnp.concatenate([hi, lo, hi, ones], axis=0)))
    a2_ref[...] = two.astype(BF16)
    c2_ref[...] = cos_two.astype(BF16)
    for h in range(2):
        col = wl_hold[:, h * BLK : h * BLK + 1]
        row = jnp.sum(col * two, axis=0, keepdims=True)
        for j in range(CHUNK // BLK):
            raw_ref[h, j : j + 1, :] = row[:, j * BLK : (j + 1) * BLK]


def filt_kernel(rank_ref, rate_ref, raw_ref, fwd_rows, cols, twist, spec_ref):
    signals = [
        (raw_ref[h] * decay_window(rate_ref, rank_ref[0], h)[0]).astype(BF16)
        for h in range(2)
    ]
    for h, spec in enumerate(forward_spectra(signals, fwd_rows, cols, twist)):
        spec_ref[h] = spec


def owner_kernel(
    rank_ref,
    taps_ref,
    skip_ref,
    rate_ref,
    w2_ref,
    wl_ref,
    recv_ref,
    raw_ref,
    spec_ref,
    fwd_rows,
    cols,
    twist,
    back_cols,
    back_rows,
    feat_any,
    a1_any,
    c1_any,
    a2_any,
    c2_any,
    back_ref,
    vec_ref,
    line_ref,
    hold_ref,
    feat_ref,
    a1_ref,
    c1_ref,
    a2_ref,
    c2_ref,
    sems,
):
    moves = [
        pltpu.make_async_copy(src, dst, sems.at[k])
        for k, (src, dst) in enumerate(
            [
                (c2_any, c2_ref),
                (c1_any, c1_ref),
                (a1_any, a1_ref),
                (feat_any.at[pl.ds(0, 48), :], feat_ref),
                (a2_any, a2_ref),
            ]
        )
    ]
    for move in moves:
        move.start()
    rank = rank_ref[0]
    hold_ref[...] = recv_ref[...].astype(F32)
    taps, gains = [], []
    xs, sides, cots, gated, grad_mixed = [], [], [], [], []
    for h in range(2):
        gains.append(picked(skip_ref[:, half(h)], rank))
        taps.append([])
        for i in range(3):
            own = picked(taps_ref[i, :, half(h)], rank)
            taps[h].append([own[m : m + 1] for m in range(3)])
        x = [hold_ref[:, i * 2 + h, :] for i in range(4)]
        shifted = [[x[i], earlier(x[i], 1), earlier(x[i], 2)] for i in range(3)]
        side = [
            taps[h][i][0] * shifted[i][0]
            + taps[h][i][1] * shifted[i][1]
            + taps[h][i][2] * shifted[i][2]
            for i in range(3)
        ]
        xs.append(shifted)
        sides.append(side)
        cots.append(x[3])
        gated.append((side[1] * side[2]).astype(BF16))
        grad_mixed.append((x[3] * side[0]).astype(BF16))
    spec = forward_spectra(gated + grad_mixed, fwd_rows, cols, twist)
    pairs = [
        [times(spec[h], spec[2 + h], True) for h in range(2)],
        [times(spec[h], spec_ref[h], False) for h in range(2)],
        [times(spec_ref[h], spec[2 + h], True) for h in range(2)],
    ]
    convs = inverse_pairs(pairs, back_cols, back_rows, twist)

    sums = []
    line_ref[...] = jnp.zeros_like(line_ref)
    for h in range(2):
        grad_filt = convs[h].astype(BF16).astype(F32)
        window, slope = decay_window(rate_ref, rank, h)
        grad_raw = grad_filt * window
        sums.append(jnp.sum(grad_raw * raw_ref[h] * slope, axis=0, keepdims=True))
        for n in range(BLK):
            line_ref[h : h + 1, n * BLK : (n + 1) * BLK] = grad_raw[n : n + 1, :]

    w2_hi, w2_lo = split(w2_ref[...])
    w2_stack = jnp.concatenate([w2_hi, w2_hi, w2_lo], axis=1)
    col0 = picked(wl_ref[:, half(0)], rank)
    col1 = picked(wl_ref[:, half(1)], rank)
    total = jnp.zeros((BLK, 192), F32)
    for move in moves:
        move.wait()
    for j in range(line_ref.shape[1] // CHUNK):
        at = slice(j * CHUNK, (j + 1) * CHUNK)
        line = line_ref[:, at]
        grad_two = (col0 * line[0:1] + col1 * line[1:2]) * c2_ref[:, at].astype(F32)
        hi, lo = split(grad_two)
        grad_one = dot(w2_stack, jnp.concatenate([hi, lo, hi], axis=0)) * c1_ref[
            :, at
        ].astype(F32)
        line_hi = line.astype(BF16).astype(F32)
        lines = jnp.concatenate([line_hi, line - line_hi], axis=0).astype(BF16)
        left = jnp.concatenate([a1_ref[:, at], feat_ref[:, at], lines], axis=0)
        right = jnp.concatenate([hi, grad_one.astype(BF16), a2_ref[:, at]], axis=0)
        total = total + dot_nt(left, right)

    shared = total[:112, :BLK]
    last = total[112:120, BLK:] + total[120:, BLK:]
    count = 33
    biases = shared[64 + ONES_ROW : 64 + ONES_ROW + 1]
    low = jnp.concatenate(
        [
            shared[64 : 64 + count, 64:],
            biases[:, 64:],
            biases[:, :64],
            jnp.zeros((64 - count - 2, 64), F32),
        ],
        axis=0,
    )
    packed = jnp.concatenate([shared[:64, :64], low], axis=1).T
    p_hi, p_lo = split(packed)
    back_ref[:, 4 * BLK : 5 * BLK] = jnp.concatenate([p_hi, p_lo], axis=1)

    lane = places()[1]
    edge = jnp.zeros((BLK, BLK), F32)
    for h in range(2):
        g = gated[h].astype(F32)
        gm = grad_mixed[h].astype(F32)
        mixed = (convs[2 + h] + gains[h] * g).astype(BF16).astype(F32)
        grad_gated = (convs[4 + h] + gains[h] * gm).astype(BF16).astype(F32)
        side = sides[h]
        grad_side = [cots[h] * mixed, grad_gated * side[2], grad_gated * side[1]]
        back_ref[:, half(h)] = mixed.astype(BF16)
        back_ref[:, half(2 + h)] = grad_gated.astype(BF16)
        sums.append(jnp.sum(gm * g, axis=0, keepdims=True))
        for i in range(3):
            at = 2 * (i * 2 + h)
            before = jnp.where(lane < 2, xs[h][i][2], 0.0)
            after = jnp.where(lane >= BLK - 2, later(grad_side[i], 2), 0.0)
            after_hi = after.astype(BF16).astype(F32)
            edge = (
                edge
                + pltpu.roll(before, at, 1)
                + pltpu.roll(after_hi, AHEAD_HI + 2 + at, 1)
                + pltpu.roll(after - after_hi, AHEAD_LO + 2 + at, 1)
            )
            for m in range(3):
                sums.append(jnp.sum(grad_side[i] * xs[h][i][m], axis=0, keepdims=True))
    back_ref[:, 5 * BLK :] = edge.astype(BF16)
    sums = jnp.concatenate(sums + [jnp.zeros((64 - len(sums), BLK), F32)], axis=0)
    totals = dot_nt(jnp.ones((8, BLK), F32), sums, lax.Precision.HIGHEST)
    vec_ref[...] = jnp.concatenate(
        [jnp.zeros((1, 64), F32), last[0:1], last[1:2], totals[0:1]], axis=1
    )


def rows_kernel(recv_ref, streams_ref, cot_ref, taps_ref, out_ref, grad_ref):
    row = places()[0]
    edge = turned(recv_ref[:, 5 * BLK :])
    for h in range(2):
        mixed = turned(recv_ref[:, half(h)])
        grad_gated = turned(recv_ref[:, half(2 + h)])
        side = []
        for i in range(3):
            at = 2 * (i * 2 + h)
            x = streams_ref[i, :, half(h)].astype(F32)
            far, near = edge[at : at + 1], edge[at + 1 : at + 2]
            one = jnp.where(row == 0, near, pltpu.roll(x, 1, 0))
            two = jnp.where(row == 0, far, jnp.where(row == 1, near, pltpu.roll(x, 2, 0)))
            side.append(
                taps_ref[i, 0:1, half(h)] * x
                + taps_ref[i, 1:2, half(h)] * one
                + taps_ref[i, 2:3, half(h)] * two
            )
        out_ref[:, half(h)] = (side[0] * mixed).astype(BF16)
        cot = cot_ref[:, half(h)].astype(F32)
        grad_side = [cot * mixed, grad_gated * side[2], grad_gated * side[1]]
        for i in range(3):
            at = 2 * (i * 2 + h)
            ahead = (
                edge[AHEAD_HI + at : AHEAD_HI + at + 2] + edge[AHEAD_LO + at : AHEAD_LO + at + 2]
            )
            near, far = ahead[0:1], ahead[1:2]
            g = grad_side[i]
            one = jnp.where(row == BLK - 1, near, pltpu.roll(g, BLK - 1, 0))
            two = jnp.where(
                row == BLK - 1,
                far,
                jnp.where(row == BLK - 2, near, pltpu.roll(g, BLK - 2, 0)),
            )
            grad_ref[i, :, half(h)] = (
                taps_ref[i, 0:1, half(h)] * g
                + taps_ref[i, 1:2, half(h)] * one
                + taps_ref[i, 2:3, half(h)] * two
            ).astype(BF16)


def final_kernel(
    all_ref, taps_ref, w1_ref, b1_ref, w2_ref, b2_ref, wl_ref, rate_ref, skip_ref
):
    low = all_ref[:, :BLK].T
    high = all_ref[:, BLK:].T
    shared = low[:64]
    flipped = shared[:, 64:]
    w2_ref[...] = shared[:, :64]
    w1_ref[...] = flipped[:33]
    b1_ref[...] = flipped[33:34]
    b2_ref[...] = flipped[34:35]
    wl_ref[:, :BLK] = low[64:]
    wl_ref[:, BLK:] = high[:64]
    rest = high[64:]
    for h in range(2):
        rate_ref[:, half(h)] = rest[h : h + 1]
        skip_ref[:, half(h)] = rest[2 + 10 * h : 3 + 10 * h]
        for i in range(3):
            at = 3 + 10 * h + 3 * i
            taps_ref[i, :, half(h)] = rest[at : at + 3]


def params(**kwargs):
    return pltpu.CompilerParams(vmem_limit_bytes=VMEM, **kwargs)


def on_device(
    streams,
    short_taps,
    w_first,
    b_first,
    w_second,
    b_second,
    w_last,
    decay_rate,
    skip_gain,
    cotangent,
):
    peers = lax.axis_size("ctx")
    rank = lax.axis_index("ctx")
    tok = streams.shape[1]
    channels = streams.shape[2]
    seq_len = tok * peers
    count, hid = w_first.shape
    vmem = pl.BlockSpec(memory_space=pltpu.VMEM)
    smem = pl.BlockSpec(memory_space=pltpu.SMEM)
    shape = jax.ShapeDtypeStruct

    row = rank.reshape(1).astype(jnp.int32)
    outgoing = pl.pallas_call(
        pack_kernel,
        out_shape=shape((peers, 8, tok), BF16),
        scratch_shapes=[pltpu.VMEM((peers, 8, tok), F32)],
        name="pack_rows",
    )(streams, cotangent)
    incoming = lax.all_to_all(outgoing, "ctx", split_axis=0, concat_axis=0, tiled=True)

    fwd_rows, cols, twist, back_cols, back_rows = (jnp.asarray(c) for c in dft_consts())
    feat = jnp.asarray(feature_const(seq_len, (count - 1) // 2))
    act = shape((hid, seq_len), BF16)
    act_spec = pl.BlockSpec((hid, CHUNK), lambda j: (0, j))
    whole = lambda *dims: pl.BlockSpec(dims, lambda j: (0,) * len(dims))
    a1, c1, a2, c2, raw = pl.pallas_call(
        net_kernel,
        grid=(seq_len // CHUNK,),
        in_specs=[
            smem,
            pl.BlockSpec((BLK, CHUNK), lambda j: (0, j)),
            whole(count, hid),
            whole(1, hid),
            whole(hid, hid),
            whole(1, hid),
            whole(hid, channels),
        ],
        out_specs=[
            act_spec,
            act_spec,
            act_spec,
            act_spec,
            pl.BlockSpec((2, CHUNK // BLK, BLK), lambda j: (0, j, 0)),
        ],
        out_shape=[act, act, act, act, shape((2, BLK, BLK), F32)],
        scratch_shapes=[
            pltpu.VMEM((hid, BLK), BF16),
            pltpu.VMEM((hid, 3 * hid + 16), BF16),
            pltpu.VMEM((hid, 2 * BLK), F32),
        ],
        compiler_params=params(dimension_semantics=("arbitrary",)),
        name="filter_net",
    )(row, feat, w_first, b_first[None], w_second, b_second[None], w_last)
    filt_spec = pl.pallas_call(
        filt_kernel,
        in_specs=[smem] + [vmem] * 5,
        out_specs=vmem,
        out_shape=shape((2, SIDE, SIDE), F32),
        compiler_params=params(),
        name="filter_spectrum",
    )(row, decay_rate[None], raw, fwd_rows, cols, twist)

    back, vec = pl.pallas_call(
        owner_kernel,
        in_specs=[smem] + [vmem] * 13 + [pl.BlockSpec(memory_space=pl.ANY)] * 5,
        out_specs=[vmem, vmem],
        out_shape=[shape((peers, 6 * tok), BF16), shape((1, 2 * BLK), F32)],
        scratch_shapes=[
            pltpu.VMEM((8, seq_len), F32),
            pltpu.VMEM((peers, 8, tok), F32),
            pltpu.VMEM((48, seq_len), BF16),
            pltpu.VMEM((hid, seq_len), BF16),
            pltpu.VMEM((hid, seq_len), BF16),
            pltpu.VMEM((hid, seq_len), BF16),
            pltpu.VMEM((hid, seq_len), BF16),
            pltpu.SemaphoreType.DMA((5,)),
        ],
        compiler_params=params(),
        name="convolve_channels",
    )(
        row,
        short_taps,
        skip_gain[None],
        decay_rate[None],
        w_second,
        w_last,
        incoming,
        raw,
        filt_spec,
        fwd_rows,
        cols,
        twist,
        back_cols,
        back_rows,
        feat,
        a1,
        c1,
        a2,
        c2,
    )
    returned = lax.all_to_all(
        back.reshape(peers, 2, 3 * tok), "ctx", split_axis=0, concat_axis=0, tiled=True
    ).reshape(peers, 6 * tok)
    returned, vec = lax.optimization_barrier((returned, vec))
    halves = jnp.sum(returned[:, 4 * tok : 5 * tok].astype(F32), axis=0)
    mine = lax.psum(halves[:64] + halves[64:], "tp")
    vec = jnp.concatenate([mine[None], vec[:, 64:]], axis=1)
    spread = jnp.broadcast_to(vec, (peers, 2 * BLK))
    gathered = lax.all_to_all(spread, "ctx", split_axis=0, concat_axis=0, tiled=True)
    output, grad_streams = pl.pallas_call(
        rows_kernel,
        out_shape=[shape((tok, channels), BF16), shape((3, tok, channels), BF16)],
        compiler_params=params(),
        name="finish_rows",
    )(returned, streams, cotangent, short_taps)
    taps, gw1, gb1, gw2, gb2, gwl, rate, skip = pl.pallas_call(
        final_kernel,
        out_shape=[
            shape((3, 3, channels), F32),
            shape((count, hid), F32),
            shape((1, hid), F32),
            shape((hid, hid), F32),
            shape((1, hid), F32),
            shape((hid, channels), F32),
            shape((1, channels), F32),
            shape((1, channels), F32),
        ],
        name="unpack_sums",
    )(gathered)
    return (
        output,
        grad_streams,
        taps,
        gw1,
        gb1[0],
        gw2,
        gb2[0],
        gwl,
        rate[0],
        skip[0],
    )


def solution(mesh):
    return jax.shard_map(
        on_device,
        mesh=mesh,
        in_specs=(
            P(None, "ctx", "tp"),
            P(None, None, "tp"),
            P(),
            P(),
            P(),
            P(),
            P(None, "tp"),
            P("tp"),
            P("tp"),
            P("ctx", "tp"),
        ),
        out_specs=(
            P("ctx", "tp"),
            P(None, "ctx", "tp"),
            P(None, None, "tp"),
            P(),
            P(),
            P(),
            P(),
            P(None, "tp"),
            P("tp"),
            P("tp"),
        ),
        check_vma=False,
    )
```

```python
import math

import jax
import jax.numpy as jnp
import ml_dtypes
import numpy as np
from jax import lax
from jax.experimental import pallas as pl
from jax.experimental.pallas import tpu as pltpu
from jax.sharding import PartitionSpec as P

F32 = jnp.float32
BF16 = jnp.bfloat16
BLK = 128
SIDE = 256
CHUNK = 2048
ONES_ROW = 33
LO_ROW = 36
HI_ROW = 69
AHEAD_HI = 16
AHEAD_LO = 32
VMEM = 56 * 1024 * 1024
NT = (((1,), (1,)), ((), ()))


def split_const(table):
    hi = table.astype(ml_dtypes.bfloat16)
    lo = (table - hi.astype(np.float64)).astype(ml_dtypes.bfloat16)
    return hi, lo


def dft_consts():
    total = SIDE * BLK
    k_row = np.arange(SIDE)[:, None]
    n_row = np.arange(BLK)[None, :]
    angle = 2 * np.pi * ((k_row * n_row) % SIDE) / SIDE
    rows = np.concatenate([np.cos(angle), -np.sin(angle)], axis=0)
    rows_hi, rows_lo = split_const(rows)
    fwd_rows = np.concatenate([rows_hi, rows_lo], axis=1)
    back_hi, back_lo = split_const(rows.T / total)
    idx = np.arange(BLK)
    angle = 2 * np.pi * ((idx[:, None] * idx[None, :]) % BLK) / BLK
    cos, sin = np.cos(angle), np.sin(angle)
    cols = np.concatenate(split_const(np.block([[cos, -sin], [sin, cos]])), axis=0)
    back_cols = np.concatenate(split_const(np.block([[cos, sin], [-sin, cos]])), axis=0)
    angle = 2 * np.pi * ((k_row * n_row) % total) / total
    twist = np.concatenate([np.cos(angle), np.sin(angle)], axis=1).astype(np.float32)
    back_rows = np.concatenate([back_hi, back_lo], axis=0)
    return fwd_rows, cols, twist, back_cols, back_rows


def feature_const(seq_len, bands):
    t = np.arange(seq_len)[None, :]
    k = np.arange(1, bands + 1)[:, None]
    angle = 2 * np.pi * ((k * t) % seq_len) / seq_len
    feat = np.concatenate([t / seq_len, np.cos(angle), np.sin(angle)], axis=0)
    hi, lo = split_const(feat)
    count = feat.shape[0]
    table = np.zeros((BLK, seq_len), ml_dtypes.bfloat16)
    table[:count] = hi
    table[ONES_ROW : ONES_ROW + 2] = 1
    table[LO_ROW : LO_ROW + count] = lo
    table[HI_ROW : HI_ROW + count] = hi
    return table


def fit_sin_cos():
    r = np.cos(np.linspace(0.0, np.pi / 2, 4001))[:-1]
    powers = np.stack([r ** (2 * i) for i in range(6)], 1)
    s = np.linalg.lstsq(powers * r[:, None], np.sin(np.pi * r), rcond=None)[0]
    c = np.linalg.lstsq(powers[:, :5], np.cos(np.pi * r), rcond=None)[0]
    return [float(v) for v in s], [float(v) for v in c]


SIN_C, COS_C = fit_sin_cos()


def sin_cos_pi(x):
    r = x - 2.0 * jnp.round(x * 0.5)
    z = r * r
    s = (SIN_C[5] * z + SIN_C[4]) * z + SIN_C[3]
    c = COS_C[4] * z + COS_C[3]
    for i in range(2, -1, -1):
        s = s * z + SIN_C[i]
        c = c * z + COS_C[i]
    return s * r, c


def split(x):
    hi = x.astype(BF16)
    return hi, (x - hi.astype(F32)).astype(BF16)


def dot(a, b):
    return jnp.dot(a, b, preferred_element_type=F32)


def dot_nt(a, b, precision=None):
    return lax.dot_general(a, b, NT, preferred_element_type=F32, precision=precision)


def eye():
    row = lax.broadcasted_iota(jnp.int32, (BLK, BLK), 0)
    col = lax.broadcasted_iota(jnp.int32, (BLK, BLK), 1)
    return jnp.where(row == col, 1.0, 0.0).astype(BF16)


def forward_spectra(signals, fwd_rows, cols, twist):
    count = len(signals)
    xs = jnp.concatenate(signals, axis=1)
    inner = dot(fwd_rows[...], jnp.concatenate([xs, xs], axis=0))
    tc, ts = twist[:, :BLK], twist[:, BLK:]
    parts = []
    for s in range(count):
        re = inner[:SIDE, s * BLK : (s + 1) * BLK]
        im = inner[SIDE:, s * BLK : (s + 1) * BLK]
        parts.append(jnp.concatenate([re * tc + im * ts, im * tc - re * ts], axis=1))
    hi, lo = split(jnp.concatenate(parts, axis=0))
    c_hi, c_lo = cols[:SIDE, :], cols[SIDE:, :]
    spec = dot(hi, c_hi) + dot(lo, c_hi) + dot(hi, c_lo)
    return [spec[s * SIDE : (s + 1) * SIDE] for s in range(count)]


def inverse_pairs(pairs, back_cols, back_rows, twist):
    joined = []
    for a, b in pairs:
        joined.append(
            jnp.concatenate([a[:, :BLK] - b[:, BLK:], a[:, BLK:] + b[:, :BLK]], axis=1)
        )
    count = len(pairs)
    hi, lo = split(jnp.concatenate(joined, axis=0))
    c_hi, c_lo = back_cols[:SIDE, :], back_cols[SIDE:, :]
    inner = dot(hi, c_hi) + dot(lo, c_hi) + dot(hi, c_lo)
    tc, ts = twist[:, :BLK], twist[:, BLK:]
    parts = []
    for s in range(count):
        re = inner[s * SIDE : (s + 1) * SIDE, :BLK]
        im = inner[s * SIDE : (s + 1) * SIDE, BLK:]
        tr = re * tc - im * ts
        ti = im * tc + re * ts
        parts.append(jnp.concatenate([tr, ti], axis=0))
        parts.append(jnp.concatenate([ti, -tr], axis=0))
    hi, lo = split(jnp.concatenate(parts, axis=1))
    r_hi, r_lo = back_rows[:BLK, :], back_rows[BLK:, :]
    out = dot(r_hi, hi) + dot(r_hi, lo) + dot(r_lo, hi)
    return [out[:, s * BLK : (s + 1) * BLK] for s in range(2 * count)]


def times(a, b, conj_a):
    ar, ai = a[:, :BLK], a[:, BLK:]
    br, bi = b[:, :BLK], b[:, BLK:]
    if conj_a:
        return jnp.concatenate([ar * br + ai * bi, ar * bi - ai * br], axis=1)
    return jnp.concatenate([ar * br - ai * bi, ar * bi + ai * br], axis=1)


def places():
    row = lax.broadcasted_iota(jnp.int32, (BLK, BLK), 0)
    col = lax.broadcasted_iota(jnp.int32, (BLK, BLK), 1)
    return row, col


def earlier(x, m):
    row, col = places()
    r = pltpu.roll(x, m, 1)
    return jnp.where(col >= m, r, jnp.where(row >= 1, pltpu.roll(r, 1, 0), 0.0))


def later(x, m):
    row, col = places()
    r = pltpu.roll(x, BLK - m, 1)
    return jnp.where(
        col < BLK - m, r, jnp.where(row < BLK - 1, pltpu.roll(r, BLK - 1, 0), 0.0)
    )


def picked(x, rank):
    lane = lax.broadcasted_iota(jnp.int32, x.shape, 1)
    return jnp.sum(jnp.where(lane == rank, x, 0.0), axis=1, keepdims=True)


def half(h):
    return slice(h * BLK, (h + 1) * BLK)


def decay_window(rate_ref, rank, h):
    row, col = places()
    t = (row * BLK + col).astype(F32)
    rate = jnp.broadcast_to(picked(rate_ref[:, half(h)], rank), (BLK, BLK))
    return jnp.sqrt(2.0 * rate) * jnp.exp(-rate * t), 0.5 / rate - t


def turned(block):
    return lax.dot_general(
        block, eye(), (((0,), (0,)), ((), ())), preferred_element_type=F32
    )


def pack_kernel(streams_ref, cot_ref, out_ref, hold_ref):
    for i in range(4):
        block = cot_ref[...] if i == 3 else streams_ref[i]
        for h in range(2):
            hold_ref[:, i * 2 + h, :] = turned(block[:, half(h)])
    out_ref[...] = hold_ref[...].astype(BF16)


def net_kernel(
    rank_ref,
    feat_ref,
    w1_ref,
    b1_ref,
    w2_ref,
    b2_ref,
    wl_ref,
    rate_ref,
    rows_any,
    cols_any,
    twist_any,
    lt_ref,
    c1_ref,
    a2_ref,
    c2_ref,
    raw_ref,
    spec_ref,
    w1_hold,
    w2_hold,
    wl_hold,
    fwd_rows,
    cols,
    twist,
    sems,
):
    step = pl.program_id(0)
    moves = [
        pltpu.make_async_copy(src, dst, sems.at[k])
        for k, (src, dst) in enumerate(
            [(rows_any, fwd_rows), (cols_any, cols), (twist_any, twist)]
        )
    ]

    @pl.when(step == 0)
    def _():
        for move in moves:
            move.start()

        def parts(ref):
            x = ref[...] * (1.0 / math.pi)
            hi = x.astype(BF16).astype(F32)
            return hi, x - hi

        w_hi, w_lo = parts(w1_ref)
        b_hi, b_lo = parts(b1_ref)
        count, hid = w_hi.shape
        gap = jnp.zeros((LO_ROW - ONES_ROW - 2, hid), F32)
        end = jnp.zeros((BLK - HI_ROW - count, hid), F32)
        stack = jnp.concatenate([w_hi, b_hi, b_lo, gap, w_hi, w_lo, end], axis=0)
        w1_hold[...] = stack.T.astype(BF16)
        w_hi, w_lo = parts(w2_ref)
        b_hi, b_lo = parts(b2_ref)
        end = jnp.zeros((14, hid), F32)
        stack = jnp.concatenate([w_hi, w_hi, w_lo, b_hi, b_lo, end], axis=0)
        w2_hold[...] = stack.T.astype(BF16)
        rank = rank_ref[0]
        for h in range(2):
            wl_hold[:, half(h)] = jnp.broadcast_to(
                picked(wl_ref[:, half(h)], rank), (hid, BLK)
            )

    one, cos_one = sin_cos_pi(dot(w1_hold[...], feat_ref[...]))
    c1_ref[...] = cos_one.astype(BF16)
    hi, lo = split(one)
    lt_ref[...] = jnp.concatenate([hi, feat_ref[0:64, :]], axis=0).T
    ones = jnp.ones((16, CHUNK), BF16)
    two, cos_two = sin_cos_pi(dot(w2_hold[...], jnp.concatenate([hi, lo, hi, ones], axis=0)))
    a2_ref[...] = two.astype(BF16)
    c2_ref[...] = cos_two.astype(BF16)
    for h in range(2):
        col = wl_hold[:, h * BLK : h * BLK + 1]
        row = jnp.sum(col * two, axis=0, keepdims=True)
        for j in range(CHUNK // BLK):
            at = step * (CHUNK // BLK) + j
            raw_ref[h, pl.ds(at, 1), :] = row[:, j * BLK : (j + 1) * BLK]

    @pl.when(step == pl.num_programs(0) - 1)
    def _():
        signals = [
            (raw_ref[h] * decay_window(rate_ref, rank_ref[0], h)[0]).astype(BF16)
            for h in range(2)
        ]
        for move in moves:
            move.wait()
        for h, spec in enumerate(forward_spectra(signals, fwd_rows, cols, twist)):
            spec_ref[h] = spec


def owner_kernel(
    rank_ref,
    taps_ref,
    skip_ref,
    rate_ref,
    w2_ref,
    wl_ref,
    recv_ref,
    *refs,
):
    large, back_ref, vec_ref, line_ref, hold_ref = refs[:11], *refs[11:15]
    copies, sems = refs[15:26], refs[26]
    fwd_rows, cols, twist, back_cols, back_rows, spec_ref, raw_ref = copies[:7]
    c2_ref, c1_ref, lt_ref, a2_ref = copies[7:]
    moves = [
        pltpu.make_async_copy(src, dst, sems.at[k])
        for k, (src, dst) in enumerate(zip(large, copies))
    ]
    for move in moves:
        move.start()
    rank = rank_ref[0]
    hold_ref[...] = recv_ref[...].astype(F32)
    taps, gains = [], []
    xs, sides, cots, gated, grad_mixed = [], [], [], [], []
    for h in range(2):
        gains.append(picked(skip_ref[:, half(h)], rank))
        taps.append([])
        for i in range(3):
            own = picked(taps_ref[i, :, half(h)], rank)
            taps[h].append([own[m : m + 1] for m in range(3)])
        x = [hold_ref[:, i * 2 + h, :] for i in range(4)]
        shifted = [[x[i], earlier(x[i], 1), earlier(x[i], 2)] for i in range(3)]
        side = [
            taps[h][i][0] * shifted[i][0]
            + taps[h][i][1] * shifted[i][1]
            + taps[h][i][2] * shifted[i][2]
            for i in range(3)
        ]
        xs.append(shifted)
        sides.append(side)
        cots.append(x[3])
        gated.append((side[1] * side[2]).astype(BF16))
        grad_mixed.append((x[3] * side[0]).astype(BF16))
    for move in moves[:7]:
        move.wait()
    spec = forward_spectra(gated + grad_mixed, fwd_rows, cols, twist)
    pairs = [
        [times(spec[h], spec[2 + h], True) for h in range(2)],
        [times(spec[h], spec_ref[h], False) for h in range(2)],
        [times(spec_ref[h], spec[2 + h], True) for h in range(2)],
    ]
    convs = inverse_pairs(pairs, back_cols, back_rows, twist)

    sums = []
    line_ref[...] = jnp.zeros_like(line_ref)
    for h in range(2):
        grad_filt = convs[h].astype(BF16).astype(F32)
        window, slope = decay_window(rate_ref, rank, h)
        grad_raw = grad_filt * window
        sums.append(jnp.sum(grad_raw * raw_ref[h] * slope, axis=0, keepdims=True))
        for n in range(BLK):
            line_ref[h : h + 1, n * BLK : (n + 1) * BLK] = grad_raw[n : n + 1, :]

    w2_hi, w2_lo = split(w2_ref[...])
    w2_stack = jnp.concatenate([w2_hi, w2_lo], axis=1)
    col0 = picked(wl_ref[:, half(0)], rank)
    col1 = picked(wl_ref[:, half(1)], rank)
    total = jnp.zeros((BLK, BLK), F32)
    last = jnp.zeros((64, 16), F32)
    for move in moves[7:]:
        move.wait()
    for j in range(line_ref.shape[1] // CHUNK):
        at = slice(j * CHUNK, (j + 1) * CHUNK)
        line = line_ref[:, at]
        grad_two = (col0 * line[0:1] + col1 * line[1:2]) * c2_ref[:, at].astype(F32)
        hi = grad_two.astype(BF16)
        grad_one = dot(w2_stack, jnp.concatenate([hi, hi], axis=0)) * c1_ref[
            :, at
        ].astype(F32)
        line_hi = line.astype(BF16).astype(F32)
        lines = jnp.concatenate([line_hi, line - line_hi], axis=0).astype(BF16)
        right = jnp.concatenate([hi, grad_one.astype(BF16)], axis=0)
        total = total + dot(right, lt_ref[at, :])
        last = last + dot_nt(a2_ref[:, at], lines)

    last = jnp.concatenate([last, jnp.zeros((64, BLK - 16), F32)], axis=1).T
    last = last[:8] + last[8:16]
    count = 33
    bias_at = slice(64 + ONES_ROW, 65 + ONES_ROW)
    low = jnp.concatenate(
        [
            total[64:, 64 : 64 + count],
            total[64:, bias_at],
            total[:64, bias_at],
            jnp.zeros((64, 64 - count - 2), F32),
        ],
        axis=1,
    )
    packed = jnp.concatenate([total[:64, :64], low], axis=0)
    p_hi, p_lo = split(packed)
    back_ref[:, 4 * BLK : 5 * BLK] = jnp.concatenate([p_hi, p_lo], axis=1)

    lane = places()[1]
    edge = jnp.zeros((BLK, BLK), F32)
    for h in range(2):
        g = gated[h].astype(F32)
        gm = grad_mixed[h].astype(F32)
        mixed = (convs[2 + h] + gains[h] * g).astype(BF16).astype(F32)
        grad_gated = (convs[4 + h] + gains[h] * gm).astype(BF16).astype(F32)
        side = sides[h]
        grad_side = [cots[h] * mixed, grad_gated * side[2], grad_gated * side[1]]
        back_ref[:, half(h)] = mixed.astype(BF16)
        back_ref[:, half(2 + h)] = grad_gated.astype(BF16)
        sums.append(jnp.sum(gm * g, axis=0, keepdims=True))
        for i in range(3):
            at = 2 * (i * 2 + h)
            before = jnp.where(lane < 2, xs[h][i][2], 0.0)
            after = jnp.where(lane >= BLK - 2, later(grad_side[i], 2), 0.0)
            after_hi = after.astype(BF16).astype(F32)
            edge = (
                edge
                + pltpu.roll(before, at, 1)
                + pltpu.roll(after_hi, AHEAD_HI + 2 + at, 1)
                + pltpu.roll(after - after_hi, AHEAD_LO + 2 + at, 1)
            )
            for m in range(3):
                sums.append(jnp.sum(grad_side[i] * xs[h][i][m], axis=0, keepdims=True))
    back_ref[:, 5 * BLK :] = edge.astype(BF16)
    sums = jnp.concatenate(sums + [jnp.zeros((64 - len(sums), BLK), F32)], axis=0)
    totals = dot_nt(jnp.ones((8, BLK), F32), sums, lax.Precision.HIGHEST)
    vec_ref[...] = jnp.concatenate(
        [jnp.zeros((1, 64), F32), last[0:1], last[1:2], totals[0:1]], axis=1
    )


def rows_kernel(recv_ref, streams_ref, cot_ref, taps_ref, out_ref, grad_ref):
    row = places()[0]
    edge = turned(recv_ref[:, 5 * BLK :])
    for h in range(2):
        mixed = turned(recv_ref[:, half(h)])
        grad_gated = turned(recv_ref[:, half(2 + h)])
        side = []
        for i in range(3):
            at = 2 * (i * 2 + h)
            x = streams_ref[i, :, half(h)].astype(F32)
            far, near = edge[at : at + 1], edge[at + 1 : at + 2]
            one = jnp.where(row == 0, near, pltpu.roll(x, 1, 0))
            two = jnp.where(row == 0, far, jnp.where(row == 1, near, pltpu.roll(x, 2, 0)))
            side.append(
                taps_ref[i, 0:1, half(h)] * x
                + taps_ref[i, 1:2, half(h)] * one
                + taps_ref[i, 2:3, half(h)] * two
            )
        out_ref[:, half(h)] = (side[0] * mixed).astype(BF16)
        cot = cot_ref[:, half(h)].astype(F32)
        grad_side = [cot * mixed, grad_gated * side[2], grad_gated * side[1]]
        for i in range(3):
            at = 2 * (i * 2 + h)
            ahead = (
                edge[AHEAD_HI + at : AHEAD_HI + at + 2] + edge[AHEAD_LO + at : AHEAD_LO + at + 2]
            )
            near, far = ahead[0:1], ahead[1:2]
            g = grad_side[i]
            one = jnp.where(row == BLK - 1, near, pltpu.roll(g, BLK - 1, 0))
            two = jnp.where(
                row == BLK - 1,
                far,
                jnp.where(row == BLK - 2, near, pltpu.roll(g, BLK - 2, 0)),
            )
            grad_ref[i, :, half(h)] = (
                taps_ref[i, 0:1, half(h)] * g
                + taps_ref[i, 1:2, half(h)] * one
                + taps_ref[i, 2:3, half(h)] * two
            ).astype(BF16)


def final_kernel(
    all_ref, taps_ref, w1_ref, b1_ref, w2_ref, b2_ref, wl_ref, rate_ref, skip_ref
):
    low = all_ref[:, 0, :BLK].T
    high = all_ref[:, 0, BLK:].T
    shared = low[:64]
    flipped = shared[:, 64:]
    w2_ref[...] = shared[:, :64]
    w1_ref[...] = flipped[:33]
    b1_ref[...] = flipped[33:34]
    b2_ref[...] = flipped[34:35]
    wl_ref[:, :BLK] = low[64:]
    wl_ref[:, BLK:] = high[:64]
    rest = high[64:]
    for h in range(2):
        rate_ref[:, half(h)] = rest[h : h + 1]
        skip_ref[:, half(h)] = rest[2 + 10 * h : 3 + 10 * h]
        for i in range(3):
            at = 3 + 10 * h + 3 * i
            taps_ref[i, :, half(h)] = rest[at : at + 3]


def params(**kwargs):
    return pltpu.CompilerParams(vmem_limit_bytes=VMEM, **kwargs)


def on_device(
    streams,
    short_taps,
    w_first,
    b_first,
    w_second,
    b_second,
    w_last,
    decay_rate,
    skip_gain,
    cotangent,
):
    peers = lax.axis_size("ctx")
    rank = lax.axis_index("ctx")
    tok = streams.shape[1]
    channels = streams.shape[2]
    seq_len = tok * peers
    count, hid = w_first.shape
    vmem = pl.BlockSpec(memory_space=pltpu.VMEM)
    smem = pl.BlockSpec(memory_space=pltpu.SMEM)
    far = pl.BlockSpec(memory_space=pl.ANY)
    shape = jax.ShapeDtypeStruct

    row = rank.reshape(1).astype(jnp.int32)
    outgoing = pl.pallas_call(
        pack_kernel,
        out_shape=shape((peers, 8, tok), BF16),
        scratch_shapes=[pltpu.VMEM((peers, 8, tok), F32)],
        name="pack_rows",
    )(streams, cotangent)
    incoming = lax.all_to_all(outgoing, "ctx", split_axis=0, concat_axis=0, tiled=True)

    fwd_rows, cols, twist, back_cols, back_rows = (jnp.asarray(c) for c in dft_consts())
    feat = jnp.asarray(feature_const(seq_len, (count - 1) // 2))
    act = shape((hid, seq_len), BF16)
    act_spec = pl.BlockSpec((hid, CHUNK), lambda j: (0, j))
    whole = lambda *dims: pl.BlockSpec(dims, lambda j: (0,) * len(dims))
    lt, c1, a2, c2, raw, filt_spec = pl.pallas_call(
        net_kernel,
        grid=(seq_len // CHUNK,),
        in_specs=[
            smem,
            pl.BlockSpec((BLK, CHUNK), lambda j: (0, j)),
            whole(count, hid),
            whole(1, hid),
            whole(hid, hid),
            whole(1, hid),
            whole(hid, channels),
            whole(1, channels),
            far,
            far,
            far,
        ],
        out_specs=[
            pl.BlockSpec((CHUNK, BLK), lambda j: (j, 0)),
            act_spec,
            act_spec,
            act_spec,
            whole(2, BLK, BLK),
            whole(2, SIDE, SIDE),
        ],
        out_shape=[shape((seq_len, BLK), BF16), act, act, act, shape((2, BLK, BLK), F32), shape((2, SIDE, SIDE), F32)],
        scratch_shapes=[
            pltpu.VMEM((hid, BLK), BF16),
            pltpu.VMEM((hid, 3 * hid + 16), BF16),
            pltpu.VMEM((hid, 2 * BLK), F32),
            pltpu.VMEM(fwd_rows.shape, BF16),
            pltpu.VMEM(cols.shape, BF16),
            pltpu.VMEM(twist.shape, F32),
            pltpu.SemaphoreType.DMA((3,)),
        ],
        compiler_params=params(dimension_semantics=("arbitrary",)),
        name="filter_net",
    )(
        row,
        feat,
        w_first,
        b_first[None],
        w_second,
        b_second[None],
        w_last,
        decay_rate[None],
        fwd_rows,
        cols,
        twist,
    )

    large = [fwd_rows, cols, twist, back_cols, back_rows, filt_spec, raw, c2, c1, lt, a2]
    back, vec = pl.pallas_call(
        owner_kernel,
        in_specs=[smem] + [vmem] * 6 + [far] * 11,
        out_specs=[vmem, vmem],
        out_shape=[shape((peers, 6 * tok), BF16), shape((1, 2 * BLK), F32)],
        scratch_shapes=[
            pltpu.VMEM((8, seq_len), F32),
            pltpu.VMEM((peers, 8, tok), F32),
            *[pltpu.VMEM(x.shape, x.dtype) for x in large],
            pltpu.SemaphoreType.DMA((len(large),)),
        ],
        compiler_params=params(),
        name="convolve_channels",
    )(
        row,
        short_taps,
        skip_gain[None],
        decay_rate[None],
        w_second,
        w_last,
        incoming,
        *large,
    )
    returned = lax.all_to_all(
        back.reshape(peers, 2, 3 * tok), "ctx", split_axis=0, concat_axis=0, tiled=True
    ).reshape(peers, 6 * tok)
    returned, vec = lax.optimization_barrier((returned, vec))
    halves = jnp.sum(returned[:, 4 * tok : 5 * tok].astype(F32), axis=0)
    mine = lax.psum(halves[:64] + halves[64:], "tp")
    vec = jnp.concatenate([mine[None], vec[:, 64:]], axis=1)
    spread = jnp.broadcast_to(vec[None], (peers, 1, 2 * BLK))
    gathered = lax.all_to_all(spread, "ctx", split_axis=0, concat_axis=0, tiled=True)
    output, grad_streams = pl.pallas_call(
        rows_kernel,
        out_shape=[shape((tok, channels), BF16), shape((3, tok, channels), BF16)],
        compiler_params=params(),
        name="finish_rows",
    )(returned, streams, cotangent, short_taps)
    taps, gw1, gb1, gw2, gb2, gwl, rate, skip = pl.pallas_call(
        final_kernel,
        out_shape=[
            shape((3, 3, channels), F32),
            shape((count, hid), F32),
            shape((1, hid), F32),
            shape((hid, hid), F32),
            shape((1, hid), F32),
            shape((hid, channels), F32),
            shape((1, channels), F32),
            shape((1, channels), F32),
        ],
        name="unpack_sums",
    )(gathered)
    return (
        output,
        grad_streams,
        taps,
        gw1,
        gb1[0],
        gw2,
        gb2[0],
        gwl,
        rate[0],
        skip[0],
    )


def solution(mesh):
    return jax.shard_map(
        on_device,
        mesh=mesh,
        in_specs=(
            P(None, "ctx", "tp"),
            P(None, None, "tp"),
            P(),
            P(),
            P(),
            P(),
            P(None, "tp"),
            P("tp"),
            P("tp"),
            P("ctx", "tp"),
        ),
        out_specs=(
            P("ctx", "tp"),
            P(None, "ctx", "tp"),
            P(None, None, "tp"),
            P(),
            P(),
            P(),
            P(),
            P(None, "tp"),
            P("tp"),
            P("tp"),
        ),
        check_vma=False,
    )
```

```python
import math

import jax
import jax.numpy as jnp
import ml_dtypes
import numpy as np
from jax import lax
from jax.experimental import pallas as pl
from jax.experimental.pallas import tpu as pltpu
from jax.sharding import PartitionSpec as P

F32 = jnp.float32
BF16 = jnp.bfloat16
BLK = 128
SIDE = 256
CHUNK = 2048
NET_CHUNK = 4096
ONES_ROW = 33
LO_ROW = 36
HI_ROW = 69
AHEAD_HI = 16
AHEAD_LO = 32
VMEM = 56 * 1024 * 1024
NT = (((1,), (1,)), ((), ()))


def split_const(table):
    hi = table.astype(ml_dtypes.bfloat16)
    lo = (table - hi.astype(np.float64)).astype(ml_dtypes.bfloat16)
    return hi, lo


def dft_consts():
    total = SIDE * BLK
    k_row = np.arange(SIDE)[:, None]
    n_row = np.arange(BLK)[None, :]
    angle = 2 * np.pi * ((k_row * n_row) % SIDE) / SIDE
    rows = np.concatenate([np.cos(angle), -np.sin(angle)], axis=0)
    rows_hi, rows_lo = split_const(rows)
    fwd_rows = np.concatenate([rows_hi, rows_lo], axis=1)
    back_hi, back_lo = split_const(rows.T / total)
    idx = np.arange(BLK)
    angle = 2 * np.pi * ((idx[:, None] * idx[None, :]) % BLK) / BLK
    cos, sin = np.cos(angle), np.sin(angle)
    cols = np.concatenate(split_const(np.block([[cos, -sin], [sin, cos]])), axis=0)
    back_cols = np.concatenate(split_const(np.block([[cos, sin], [-sin, cos]])), axis=0)
    angle = 2 * np.pi * ((k_row * n_row) % total) / total
    twist = np.concatenate([np.cos(angle), np.sin(angle)], axis=1).astype(np.float32)
    back_rows = np.concatenate([back_hi, back_lo], axis=0)
    return fwd_rows, cols, twist, back_cols, back_rows


def feature_const(seq_len, bands):
    t = np.arange(seq_len)[None, :]
    k = np.arange(1, bands + 1)[:, None]
    angle = 2 * np.pi * ((k * t) % seq_len) / seq_len
    feat = np.concatenate([t / seq_len, np.cos(angle), np.sin(angle)], axis=0)
    hi, lo = split_const(feat)
    count = feat.shape[0]
    table = np.zeros((BLK, seq_len), ml_dtypes.bfloat16)
    table[:count] = hi
    table[ONES_ROW : ONES_ROW + 2] = 1
    table[LO_ROW : LO_ROW + count] = lo
    table[HI_ROW : HI_ROW + count] = hi
    return table


def fit_sin_cos():
    r = np.cos(np.linspace(0.0, np.pi / 2, 4001))[:-1]
    powers = np.stack([r ** (2 * i) for i in range(6)], 1)
    s = np.linalg.lstsq(powers[:, :5] * r[:, None], np.sin(np.pi * r), rcond=None)[0]
    c = np.linalg.lstsq(powers[:, :5], np.cos(np.pi * r), rcond=None)[0]
    return [float(v) for v in s], [float(v) for v in c]


SIN_C, COS_C = fit_sin_cos()


def sin_cos_pi(x):
    r = x - 2.0 * jnp.round(x * 0.5)
    z = r * r
    s = SIN_C[4] * z + SIN_C[3]
    c = COS_C[4] * z + COS_C[3]
    for i in range(2, -1, -1):
        s = s * z + SIN_C[i]
        c = c * z + COS_C[i]
    return s * r, c


def split(x):
    hi = x.astype(BF16)
    return hi, (x - hi.astype(F32)).astype(BF16)


def dot(a, b):
    return jnp.dot(a, b, preferred_element_type=F32)


def dot_nt(a, b, precision=None):
    return lax.dot_general(a, b, NT, preferred_element_type=F32, precision=precision)


def eye():
    row = lax.broadcasted_iota(jnp.int32, (BLK, BLK), 0)
    col = lax.broadcasted_iota(jnp.int32, (BLK, BLK), 1)
    return jnp.where(row == col, 1.0, 0.0).astype(BF16)


def forward_spectra(signals, fwd_rows, cols, twist):
    count = len(signals)
    xs = jnp.concatenate(signals, axis=1)
    inner = dot(fwd_rows[...], jnp.concatenate([xs, xs], axis=0))
    tc, ts = twist[:, :BLK], twist[:, BLK:]
    parts = []
    for s in range(count):
        re = inner[:SIDE, s * BLK : (s + 1) * BLK]
        im = inner[SIDE:, s * BLK : (s + 1) * BLK]
        parts.append(jnp.concatenate([re * tc + im * ts, im * tc - re * ts], axis=1))
    hi, lo = split(jnp.concatenate(parts, axis=0))
    c_hi, c_lo = cols[:SIDE, :], cols[SIDE:, :]
    spec = dot(hi, c_hi) + dot(lo, c_hi) + dot(hi, c_lo)
    return [spec[s * SIDE : (s + 1) * SIDE] for s in range(count)]


def inverse_pairs(pairs, back_cols, back_rows, twist):
    joined = []
    for a, b in pairs:
        joined.append(
            jnp.concatenate([a[:, :BLK] - b[:, BLK:], a[:, BLK:] + b[:, :BLK]], axis=1)
        )
    count = len(pairs)
    hi, lo = split(jnp.concatenate(joined, axis=0))
    c_hi, c_lo = back_cols[:SIDE, :], back_cols[SIDE:, :]
    inner = dot(hi, c_hi) + dot(lo, c_hi) + dot(hi, c_lo)
    tc, ts = twist[:, :BLK], twist[:, BLK:]
    parts = []
    for s in range(count):
        re = inner[s * SIDE : (s + 1) * SIDE, :BLK]
        im = inner[s * SIDE : (s + 1) * SIDE, BLK:]
        tr = re * tc - im * ts
        ti = im * tc + re * ts
        parts.append(jnp.concatenate([tr, ti], axis=0))
        parts.append(jnp.concatenate([ti, -tr], axis=0))
    hi, lo = split(jnp.concatenate(parts, axis=1))
    r_hi, r_lo = back_rows[:BLK, :], back_rows[BLK:, :]
    out = dot(r_hi, hi) + dot(r_hi, lo) + dot(r_lo, hi)
    return [out[:, s * BLK : (s + 1) * BLK] for s in range(2 * count)]


def times(a, b, conj_a):
    ar, ai = a[:, :BLK], a[:, BLK:]
    br, bi = b[:, :BLK], b[:, BLK:]
    if conj_a:
        return jnp.concatenate([ar * br + ai * bi, ar * bi - ai * br], axis=1)
    return jnp.concatenate([ar * br - ai * bi, ar * bi + ai * br], axis=1)


def places():
    row = lax.broadcasted_iota(jnp.int32, (BLK, BLK), 0)
    col = lax.broadcasted_iota(jnp.int32, (BLK, BLK), 1)
    return row, col


def earlier(x, m):
    row, col = places()
    r = pltpu.roll(x, m, 1)
    return jnp.where(col >= m, r, jnp.where(row >= 1, pltpu.roll(r, 1, 0), 0.0))


def later(x, m):
    row, col = places()
    r = pltpu.roll(x, BLK - m, 1)
    return jnp.where(
        col < BLK - m, r, jnp.where(row < BLK - 1, pltpu.roll(r, BLK - 1, 0), 0.0)
    )


def picked(x, rank):
    lane = lax.broadcasted_iota(jnp.int32, x.shape, 1)
    return jnp.sum(jnp.where(lane == rank, x, 0.0), axis=1, keepdims=True)


def half(h):
    return slice(h * BLK, (h + 1) * BLK)


def decay_window(rate_ref, rank, h):
    row, col = places()
    t = (row * BLK + col).astype(F32)
    rate = jnp.broadcast_to(picked(rate_ref[:, half(h)], rank), (BLK, BLK))
    return jnp.sqrt(2.0 * rate) * jnp.exp(-rate * t), 0.5 / rate - t


def turned(block):
    return lax.dot_general(
        block, eye(), (((0,), (0,)), ((), ())), preferred_element_type=F32
    )


def pack_kernel(streams_ref, cot_ref, out_ref, hold_ref):
    for i in range(4):
        block = cot_ref[...] if i == 3 else streams_ref[i]
        for h in range(2):
            hold_ref[:, i * 2 + h, :] = turned(block[:, half(h)])
    out_ref[...] = hold_ref[...].astype(BF16)


def net_kernel(
    rank_ref,
    feat_ref,
    w1_ref,
    b1_ref,
    w2_ref,
    b2_ref,
    wl_ref,
    rate_ref,
    rows_any,
    cols_any,
    twist_any,
    lt_ref,
    c1_ref,
    a2_ref,
    c2_ref,
    raw_ref,
    spec_ref,
    w1_hold,
    w2_hold,
    wl_hold,
    fwd_rows,
    cols,
    twist,
    sems,
):
    step = pl.program_id(0)
    moves = [
        pltpu.make_async_copy(src, dst, sems.at[k])
        for k, (src, dst) in enumerate(
            [(rows_any, fwd_rows), (cols_any, cols), (twist_any, twist)]
        )
    ]

    @pl.when(step == 0)
    def _():
        for move in moves:
            move.start()

        def parts(ref):
            x = ref[...] * (1.0 / math.pi)
            hi = x.astype(BF16).astype(F32)
            return hi, x - hi

        w_hi, w_lo = parts(w1_ref)
        b_hi, b_lo = parts(b1_ref)
        count, hid = w_hi.shape
        gap = jnp.zeros((LO_ROW - ONES_ROW - 2, hid), F32)
        end = jnp.zeros((BLK - HI_ROW - count, hid), F32)
        stack = jnp.concatenate([w_hi, b_hi, b_lo, gap, w_hi, w_lo, end], axis=0)
        w1_hold[...] = stack.T.astype(BF16)
        w_hi, w_lo = parts(w2_ref)
        b_hi, b_lo = parts(b2_ref)
        end = jnp.zeros((14, hid), F32)
        stack = jnp.concatenate([w_hi, w_hi, w_lo, b_hi, b_lo, end], axis=0)
        w2_hold[...] = stack.T.astype(BF16)
        rank = rank_ref[0]
        for h in range(2):
            wl_hold[:, half(h)] = jnp.broadcast_to(
                picked(wl_ref[:, half(h)], rank), (hid, BLK)
            )

    one, cos_one = sin_cos_pi(dot(w1_hold[...], feat_ref[...]))
    c1_ref[...] = cos_one.astype(BF16)
    hi, lo = split(one)
    lt_ref[...] = jnp.concatenate([hi, feat_ref[0:64, :]], axis=0).T
    ones = jnp.ones((16, NET_CHUNK), BF16)
    two, cos_two = sin_cos_pi(dot(w2_hold[...], jnp.concatenate([hi, lo, hi, ones], axis=0)))
    a2_ref[...] = two.astype(BF16)
    c2_ref[...] = cos_two.astype(BF16)
    for h in range(2):
        col = wl_hold[:, h * BLK : h * BLK + 1]
        row = jnp.sum(col * two, axis=0, keepdims=True)
        for j in range(NET_CHUNK // BLK):
            at = step * (NET_CHUNK // BLK) + j
            raw_ref[h, pl.ds(at, 1), :] = row[:, j * BLK : (j + 1) * BLK]

    @pl.when(step == pl.num_programs(0) - 1)
    def _():
        signals = [
            (raw_ref[h] * decay_window(rate_ref, rank_ref[0], h)[0]).astype(BF16)
            for h in range(2)
        ]
        for move in moves:
            move.wait()
        for h, spec in enumerate(forward_spectra(signals, fwd_rows, cols, twist)):
            spec_ref[h] = spec


def owner_kernel(
    rank_ref,
    taps_ref,
    skip_ref,
    rate_ref,
    w2_ref,
    wl_ref,
    recv_ref,
    *refs,
):
    large, back_ref, vec_ref, line_ref, hold_ref = refs[:11], *refs[11:15]
    copies, sems = refs[15:26], refs[26]
    fwd_rows, cols, twist, back_cols, back_rows, spec_ref, raw_ref = copies[:7]
    c2_ref, c1_ref, lt_ref, a2_ref = copies[7:]
    moves = [
        pltpu.make_async_copy(src, dst, sems.at[k])
        for k, (src, dst) in enumerate(zip(large, copies))
    ]
    for move in moves:
        move.start()
    rank = rank_ref[0]
    hold_ref[...] = recv_ref[...].astype(F32)
    taps, gains = [], []
    xs, sides, cots, gated, grad_mixed = [], [], [], [], []
    for h in range(2):
        gains.append(picked(skip_ref[:, half(h)], rank))
        taps.append([])
        for i in range(3):
            own = picked(taps_ref[i, :, half(h)], rank)
            taps[h].append([own[m : m + 1] for m in range(3)])
        x = [hold_ref[:, i * 2 + h, :] for i in range(4)]
        shifted = [[x[i], earlier(x[i], 1), earlier(x[i], 2)] for i in range(3)]
        side = [
            taps[h][i][0] * shifted[i][0]
            + taps[h][i][1] * shifted[i][1]
            + taps[h][i][2] * shifted[i][2]
            for i in range(3)
        ]
        xs.append(shifted)
        sides.append(side)
        cots.append(x[3])
        gated.append((side[1] * side[2]).astype(BF16))
        grad_mixed.append((x[3] * side[0]).astype(BF16))
    for move in moves[:7]:
        move.wait()
    spec = forward_spectra(gated + grad_mixed, fwd_rows, cols, twist)
    pairs = [
        [times(spec[h], spec[2 + h], True) for h in range(2)],
        [times(spec[h], spec_ref[h], False) for h in range(2)],
        [times(spec_ref[h], spec[2 + h], True) for h in range(2)],
    ]
    convs = inverse_pairs(pairs, back_cols, back_rows, twist)

    sums = []
    line_ref[...] = jnp.zeros_like(line_ref)
    for h in range(2):
        grad_filt = convs[h].astype(BF16).astype(F32)
        window, slope = decay_window(rate_ref, rank, h)
        grad_raw = grad_filt * window
        sums.append(jnp.sum(grad_raw * raw_ref[h] * slope, axis=0, keepdims=True))
        for n in range(BLK):
            line_ref[h : h + 1, n * BLK : (n + 1) * BLK] = grad_raw[n : n + 1, :]

    w2_hi, w2_lo = split(w2_ref[...])
    w2_stack = jnp.concatenate([w2_hi, w2_lo], axis=1)
    col0 = picked(wl_ref[:, half(0)], rank)
    col1 = picked(wl_ref[:, half(1)], rank)
    total = jnp.zeros((BLK, BLK), F32)
    last = jnp.zeros((64, 16), F32)
    for move in moves[7:]:
        move.wait()
    for j in range(line_ref.shape[1] // CHUNK):
        at = slice(j * CHUNK, (j + 1) * CHUNK)
        line = line_ref[:, at]
        grad_two = (col0 * line[0:1] + col1 * line[1:2]) * c2_ref[:, at].astype(F32)
        hi = grad_two.astype(BF16)
        grad_one = dot(w2_stack, jnp.concatenate([hi, hi], axis=0)) * c1_ref[
            :, at
        ].astype(F32)
        line_hi = line.astype(BF16).astype(F32)
        lines = jnp.concatenate([line_hi, line - line_hi], axis=0).astype(BF16)
        right = jnp.concatenate([hi, grad_one.astype(BF16)], axis=0)
        total = total + dot(right, lt_ref[at, :])
        last = last + dot_nt(a2_ref[:, at], lines)

    last = jnp.concatenate([last, jnp.zeros((64, BLK - 16), F32)], axis=1).T
    last = last[:8] + last[8:16]
    count = 33
    bias_at = slice(64 + ONES_ROW, 65 + ONES_ROW)
    low = jnp.concatenate(
        [
            total[64:, 64 : 64 + count],
            total[64:, bias_at],
            total[:64, bias_at],
            jnp.zeros((64, 64 - count - 2), F32),
        ],
        axis=1,
    )
    packed = jnp.concatenate([total[:64, :64], low], axis=0)
    p_hi, p_lo = split(packed)
    rows = [None] * 6
    rows[4] = jnp.concatenate([p_hi, p_lo], axis=1)

    lane = places()[1]
    edge = jnp.zeros((BLK, BLK), F32)
    for h in range(2):
        g = gated[h].astype(F32)
        gm = grad_mixed[h].astype(F32)
        mixed = (convs[2 + h] + gains[h] * g).astype(BF16).astype(F32)
        grad_gated = (convs[4 + h] + gains[h] * gm).astype(BF16).astype(F32)
        side = sides[h]
        grad_side = [cots[h] * mixed, grad_gated * side[2], grad_gated * side[1]]
        rows[h] = mixed
        rows[2 + h] = grad_gated
        sums.append(jnp.sum(gm * g, axis=0, keepdims=True))
        for i in range(3):
            at = 2 * (i * 2 + h)
            before = jnp.where(lane < 2, xs[h][i][2], 0.0)
            after = jnp.where(lane >= BLK - 2, later(grad_side[i], 2), 0.0)
            after_hi = after.astype(BF16).astype(F32)
            edge = (
                edge
                + pltpu.roll(before, at, 1)
                + pltpu.roll(after_hi, AHEAD_HI + 2 + at, 1)
                + pltpu.roll(after - after_hi, AHEAD_LO + 2 + at, 1)
            )
            for m in range(3):
                sums.append(jnp.sum(grad_side[i] * xs[h][i][m], axis=0, keepdims=True))
    rows[5] = edge
    for k in range(3):
        pair = [rows[k].astype(F32), rows[3 + k].astype(F32)]
        back_ref[:, :, half(k)] = jnp.stack(pair, axis=1).astype(BF16)
    sums = jnp.concatenate(sums + [jnp.zeros((64 - len(sums), BLK), F32)], axis=0)
    totals = dot_nt(jnp.ones((8, BLK), F32), sums, lax.Precision.HIGHEST)
    vec_ref[...] = jnp.concatenate(
        [jnp.zeros((1, 64), F32), last[0:1], last[1:2], totals[0:1]], axis=1
    )


def rows_kernel(recv_ref, streams_ref, cot_ref, taps_ref, out_ref, grad_ref):
    row = places()[0]
    edge = turned(recv_ref[:, 5 * BLK :])
    for h in range(2):
        mixed = turned(recv_ref[:, half(h)])
        grad_gated = turned(recv_ref[:, half(2 + h)])
        side = []
        for i in range(3):
            at = 2 * (i * 2 + h)
            x = streams_ref[i, :, half(h)].astype(F32)
            far, near = edge[at : at + 1], edge[at + 1 : at + 2]
            one = jnp.where(row == 0, near, pltpu.roll(x, 1, 0))
            two = jnp.where(row == 0, far, jnp.where(row == 1, near, pltpu.roll(x, 2, 0)))
            side.append(
                taps_ref[i, 0:1, half(h)] * x
                + taps_ref[i, 1:2, half(h)] * one
                + taps_ref[i, 2:3, half(h)] * two
            )
        out_ref[:, half(h)] = (side[0] * mixed).astype(BF16)
        cot = cot_ref[:, half(h)].astype(F32)
        grad_side = [cot * mixed, grad_gated * side[2], grad_gated * side[1]]
        for i in range(3):
            at = 2 * (i * 2 + h)
            ahead = (
                edge[AHEAD_HI + at : AHEAD_HI + at + 2] + edge[AHEAD_LO + at : AHEAD_LO + at + 2]
            )
            near, far = ahead[0:1], ahead[1:2]
            g = grad_side[i]
            one = jnp.where(row == BLK - 1, near, pltpu.roll(g, BLK - 1, 0))
            two = jnp.where(
                row == BLK - 1,
                far,
                jnp.where(row == BLK - 2, near, pltpu.roll(g, BLK - 2, 0)),
            )
            grad_ref[i, :, half(h)] = (
                taps_ref[i, 0:1, half(h)] * g
                + taps_ref[i, 1:2, half(h)] * one
                + taps_ref[i, 2:3, half(h)] * two
            ).astype(BF16)


def final_kernel(
    all_ref, taps_ref, w1_ref, b1_ref, w2_ref, b2_ref, wl_ref, rate_ref, skip_ref
):
    low = all_ref[:, 0, :BLK].T
    high = all_ref[:, 0, BLK:].T
    shared = low[:64]
    flipped = shared[:, 64:]
    w2_ref[...] = shared[:, :64]
    w1_ref[...] = flipped[:33]
    b1_ref[...] = flipped[33:34]
    b2_ref[...] = flipped[34:35]
    wl_ref[:, :BLK] = low[64:]
    wl_ref[:, BLK:] = high[:64]
    rest = high[64:]
    for h in range(2):
        rate_ref[:, half(h)] = rest[h : h + 1]
        skip_ref[:, half(h)] = rest[2 + 10 * h : 3 + 10 * h]
        for i in range(3):
            at = 3 + 10 * h + 3 * i
            taps_ref[i, :, half(h)] = rest[at : at + 3]


def params(**kwargs):
    return pltpu.CompilerParams(vmem_limit_bytes=VMEM, **kwargs)


def on_device(
    streams,
    short_taps,
    w_first,
    b_first,
    w_second,
    b_second,
    w_last,
    decay_rate,
    skip_gain,
    cotangent,
):
    peers = lax.axis_size("ctx")
    rank = lax.axis_index("ctx")
    tok = streams.shape[1]
    channels = streams.shape[2]
    seq_len = tok * peers
    count, hid = w_first.shape
    vmem = pl.BlockSpec(memory_space=pltpu.VMEM)
    smem = pl.BlockSpec(memory_space=pltpu.SMEM)
    far = pl.BlockSpec(memory_space=pl.ANY)
    shape = jax.ShapeDtypeStruct

    row = rank.reshape(1).astype(jnp.int32)
    outgoing = pl.pallas_call(
        pack_kernel,
        out_shape=shape((peers, 8, tok), BF16),
        scratch_shapes=[pltpu.VMEM((peers, 8, tok), F32)],
        name="pack_rows",
    )(streams, cotangent)
    incoming = lax.all_to_all(outgoing, "ctx", split_axis=0, concat_axis=0, tiled=True)

    fwd_rows, cols, twist, back_cols, back_rows = (jnp.asarray(c) for c in dft_consts())
    feat = jnp.asarray(feature_const(seq_len, (count - 1) // 2))
    act = shape((hid, seq_len), BF16)
    act_spec = pl.BlockSpec((hid, NET_CHUNK), lambda j: (0, j))
    whole = lambda *dims: pl.BlockSpec(dims, lambda j: (0,) * len(dims))
    lt, c1, a2, c2, raw, filt_spec = pl.pallas_call(
        net_kernel,
        grid=(seq_len // NET_CHUNK,),
        in_specs=[
            smem,
            pl.BlockSpec((BLK, NET_CHUNK), lambda j: (0, j)),
            whole(count, hid),
            whole(1, hid),
            whole(hid, hid),
            whole(1, hid),
            whole(hid, channels),
            whole(1, channels),
            far,
            far,
            far,
        ],
        out_specs=[
            pl.BlockSpec((NET_CHUNK, BLK), lambda j: (j, 0)),
            act_spec,
            act_spec,
            act_spec,
            whole(2, BLK, BLK),
            whole(2, SIDE, SIDE),
        ],
        out_shape=[shape((seq_len, BLK), BF16), act, act, act, shape((2, BLK, BLK), F32), shape((2, SIDE, SIDE), F32)],
        scratch_shapes=[
            pltpu.VMEM((hid, BLK), BF16),
            pltpu.VMEM((hid, 3 * hid + 16), BF16),
            pltpu.VMEM((hid, 2 * BLK), F32),
            pltpu.VMEM(fwd_rows.shape, BF16),
            pltpu.VMEM(cols.shape, BF16),
            pltpu.VMEM(twist.shape, F32),
            pltpu.SemaphoreType.DMA((3,)),
        ],
        compiler_params=params(dimension_semantics=("arbitrary",)),
        name="filter_net",
    )(
        row,
        feat,
        w_first,
        b_first[None],
        w_second,
        b_second[None],
        w_last,
        decay_rate[None],
        fwd_rows,
        cols,
        twist,
    )

    large = [fwd_rows, cols, twist, back_cols, back_rows, filt_spec, raw, c2, c1, lt, a2]
    back, vec = pl.pallas_call(
        owner_kernel,
        in_specs=[smem] + [vmem] * 6 + [far] * 11,
        out_specs=[vmem, vmem],
        out_shape=[shape((peers, 2, 3 * tok), BF16), shape((1, 2 * BLK), F32)],
        scratch_shapes=[
            pltpu.VMEM((8, seq_len), F32),
            pltpu.VMEM((peers, 8, tok), F32),
            *[pltpu.VMEM(x.shape, x.dtype) for x in large],
            pltpu.SemaphoreType.DMA((len(large),)),
        ],
        compiler_params=params(),
        name="convolve_channels",
    )(
        row,
        short_taps,
        skip_gain[None],
        decay_rate[None],
        w_second,
        w_last,
        incoming,
        *large,
    )
    returned = lax.all_to_all(back, "ctx", split_axis=0, concat_axis=0, tiled=True)
    returned, vec = lax.optimization_barrier((returned, vec))
    halves = jnp.sum(returned[:, 1, tok : 2 * tok].astype(F32), axis=0)
    returned = returned.reshape(peers, 6 * tok)
    mine = lax.psum(halves[:64] + halves[64:], "tp")
    vec = jnp.concatenate([mine[None], vec[:, 64:]], axis=1)
    spread = jnp.broadcast_to(vec[None], (peers, 1, 2 * BLK))
    gathered = lax.all_to_all(spread, "ctx", split_axis=0, concat_axis=0, tiled=True)
    output, grad_streams = pl.pallas_call(
        rows_kernel,
        out_shape=[shape((tok, channels), BF16), shape((3, tok, channels), BF16)],
        compiler_params=params(),
        name="finish_rows",
    )(returned, streams, cotangent, short_taps)
    taps, gw1, gb1, gw2, gb2, gwl, rate, skip = pl.pallas_call(
        final_kernel,
        out_shape=[
            shape((3, 3, channels), F32),
            shape((count, hid), F32),
            shape((1, hid), F32),
            shape((hid, hid), F32),
            shape((1, hid), F32),
            shape((hid, channels), F32),
            shape((1, channels), F32),
            shape((1, channels), F32),
        ],
        name="unpack_sums",
    )(gathered)
    return (
        output,
        grad_streams,
        taps,
        gw1,
        gb1[0],
        gw2,
        gb2[0],
        gwl,
        rate[0],
        skip[0],
    )


def solution(mesh):
    return jax.shard_map(
        on_device,
        mesh=mesh,
        in_specs=(
            P(None, "ctx", "tp"),
            P(None, None, "tp"),
            P(),
            P(),
            P(),
            P(),
            P(None, "tp"),
            P("tp"),
            P("tp"),
            P("ctx", "tp"),
        ),
        out_specs=(
            P("ctx", "tp"),
            P(None, "ctx", "tp"),
            P(None, None, "tp"),
            P(),
            P(),
            P(),
            P(),
            P(None, "tp"),
            P("tp"),
            P("tp"),
        ),
        check_vma=False,
    )
```

```python
import math

import jax
import jax.numpy as jnp
import ml_dtypes
import numpy as np
from jax import lax
from jax.experimental import pallas as pl
from jax.experimental.pallas import tpu as pltpu
from jax.sharding import PartitionSpec as P

F32 = jnp.float32
BF16 = jnp.bfloat16
BLK = 128
SIDE = 256
CHUNK = 2048
NET_CHUNK = 4096
ONES_ROW = 33
LO_ROW = 36
HI_ROW = 69
AHEAD_HI = 16
AHEAD_LO = 32
VMEM = 56 * 1024 * 1024
NT = (((1,), (1,)), ((), ()))


def split_const(table):
    hi = table.astype(ml_dtypes.bfloat16)
    lo = (table - hi.astype(np.float64)).astype(ml_dtypes.bfloat16)
    return hi, lo


def dft_consts():
    total = SIDE * BLK
    k_row = np.arange(SIDE)[:, None]
    n_row = np.arange(BLK)[None, :]
    angle = 2 * np.pi * ((k_row * n_row) % SIDE) / SIDE
    rows = np.concatenate([np.cos(angle), -np.sin(angle)], axis=0)
    rows_hi, rows_lo = split_const(rows)
    fwd_rows = np.concatenate([rows_hi, rows_lo], axis=1)
    back_hi, back_lo = split_const(rows.T / total)
    idx = np.arange(BLK)
    angle = 2 * np.pi * ((idx[:, None] * idx[None, :]) % BLK) / BLK
    cos, sin = np.cos(angle), np.sin(angle)
    cols = np.concatenate(split_const(np.block([[cos, -sin], [sin, cos]])), axis=0)
    back_cols = np.concatenate(split_const(np.block([[cos, sin], [-sin, cos]])), axis=0)
    angle = 2 * np.pi * ((k_row * n_row) % total) / total
    twist = np.concatenate([np.cos(angle), np.sin(angle)], axis=1).astype(np.float32)
    back_rows = np.concatenate([back_hi, back_lo], axis=0)
    return fwd_rows, cols, twist, back_cols, back_rows


def feature_const(seq_len, bands):
    t = np.arange(seq_len)[None, :]
    k = np.arange(1, bands + 1)[:, None]
    angle = 2 * np.pi * ((k * t) % seq_len) / seq_len
    feat = np.concatenate([t / seq_len, np.cos(angle), np.sin(angle)], axis=0)
    hi, lo = split_const(feat)
    count = feat.shape[0]
    table = np.zeros((BLK, seq_len), ml_dtypes.bfloat16)
    table[:count] = hi
    table[ONES_ROW : ONES_ROW + 2] = 1
    table[LO_ROW : LO_ROW + count] = lo
    table[HI_ROW : HI_ROW + count] = hi
    return table


def fit_sin_cos():
    r = np.cos(np.linspace(0.0, np.pi / 2, 4001))[:-1]
    powers = np.stack([r ** (2 * i) for i in range(6)], 1)
    s = np.linalg.lstsq(powers[:, :5] * r[:, None], np.sin(np.pi * r), rcond=None)[0]
    c = np.linalg.lstsq(powers[:, :5], np.cos(np.pi * r), rcond=None)[0]
    return [float(v) for v in s], [float(v) for v in c]


SIN_C, COS_C = fit_sin_cos()


def sin_cos_pi(x):
    r = x - 2.0 * jnp.round(x * 0.5)
    z = r * r
    s = SIN_C[4] * z + SIN_C[3]
    c = COS_C[4] * z + COS_C[3]
    for i in range(2, -1, -1):
        s = s * z + SIN_C[i]
        c = c * z + COS_C[i]
    return s * r, c


def split(x):
    hi = x.astype(BF16)
    return hi, (x - hi.astype(F32)).astype(BF16)


def dot(a, b):
    return jnp.dot(a, b, preferred_element_type=F32)


def dot_nt(a, b, precision=None):
    return lax.dot_general(a, b, NT, preferred_element_type=F32, precision=precision)


def eye():
    row = lax.broadcasted_iota(jnp.int32, (BLK, BLK), 0)
    col = lax.broadcasted_iota(jnp.int32, (BLK, BLK), 1)
    return jnp.where(row == col, 1.0, 0.0).astype(BF16)


def forward_spectra(signals, fwd_rows, cols, twist):
    count = len(signals)
    xs = jnp.concatenate(signals, axis=1)
    inner = dot(fwd_rows[...], jnp.concatenate([xs, xs], axis=0))
    tc, ts = twist[:, :BLK], twist[:, BLK:]
    parts = []
    for s in range(count):
        re = inner[:SIDE, s * BLK : (s + 1) * BLK]
        im = inner[SIDE:, s * BLK : (s + 1) * BLK]
        parts.append(jnp.concatenate([re * tc + im * ts, im * tc - re * ts], axis=1))
    hi, lo = split(jnp.concatenate(parts, axis=0))
    c_hi, c_lo = cols[:SIDE, :], cols[SIDE:, :]
    spec = dot(hi, c_hi) + dot(lo, c_hi) + dot(hi, c_lo)
    return [spec[s * SIDE : (s + 1) * SIDE] for s in range(count)]


def inverse_pairs(pairs, back_cols, back_rows, twist):
    joined = []
    for a, b in pairs:
        joined.append(
            jnp.concatenate([a[:, :BLK] - b[:, BLK:], a[:, BLK:] + b[:, :BLK]], axis=1)
        )
    count = len(pairs)
    hi, lo = split(jnp.concatenate(joined, axis=0))
    c_hi, c_lo = back_cols[:SIDE, :], back_cols[SIDE:, :]
    inner = dot(hi, c_hi) + dot(lo, c_hi) + dot(hi, c_lo)
    tc, ts = twist[:, :BLK], twist[:, BLK:]
    parts = []
    for s in range(count):
        re = inner[s * SIDE : (s + 1) * SIDE, :BLK]
        im = inner[s * SIDE : (s + 1) * SIDE, BLK:]
        tr = re * tc - im * ts
        ti = im * tc + re * ts
        parts.append(jnp.concatenate([tr, ti], axis=0))
        parts.append(jnp.concatenate([ti, -tr], axis=0))
    hi, lo = split(jnp.concatenate(parts, axis=1))
    r_hi, r_lo = back_rows[:BLK, :], back_rows[BLK:, :]
    out = dot(r_hi, hi) + dot(r_hi, lo) + dot(r_lo, hi)
    return [out[:, s * BLK : (s + 1) * BLK] for s in range(2 * count)]


def times(a, b, conj_a):
    ar, ai = a[:, :BLK], a[:, BLK:]
    br, bi = b[:, :BLK], b[:, BLK:]
    if conj_a:
        return jnp.concatenate([ar * br + ai * bi, ar * bi - ai * br], axis=1)
    return jnp.concatenate([ar * br - ai * bi, ar * bi + ai * br], axis=1)


def places():
    row = lax.broadcasted_iota(jnp.int32, (BLK, BLK), 0)
    col = lax.broadcasted_iota(jnp.int32, (BLK, BLK), 1)
    return row, col


def earlier(x, m):
    row, col = places()
    r = pltpu.roll(x, m, 1)
    return jnp.where(col >= m, r, jnp.where(row >= 1, pltpu.roll(r, 1, 0), 0.0))


def later(x, m):
    row, col = places()
    r = pltpu.roll(x, BLK - m, 1)
    return jnp.where(
        col < BLK - m, r, jnp.where(row < BLK - 1, pltpu.roll(r, BLK - 1, 0), 0.0)
    )


def picked(x, rank):
    lane = lax.broadcasted_iota(jnp.int32, x.shape, 1)
    return jnp.sum(jnp.where(lane == rank, x, 0.0), axis=1, keepdims=True)


def half(h):
    return slice(h * BLK, (h + 1) * BLK)


def decay_window(rate_ref, rank, h):
    row, col = places()
    t = (row * BLK + col).astype(F32)
    rate = jnp.broadcast_to(picked(rate_ref[:, half(h)], rank), (BLK, BLK))
    return jnp.sqrt(2.0 * rate) * jnp.exp(-rate * t), 0.5 / rate - t


def turned(block):
    return lax.dot_general(
        block, eye(), (((0,), (0,)), ((), ())), preferred_element_type=F32
    )


def pack_kernel(streams_ref, cot_ref, out_ref, hold_ref):
    for i in range(4):
        block = cot_ref[...] if i == 3 else streams_ref[i]
        for h in range(2):
            hold_ref[:, i * 2 + h, :] = turned(block[:, half(h)])
    out_ref[...] = hold_ref[...].astype(BF16)


def net_kernel(
    rank_ref,
    feat_ref,
    w1_ref,
    b1_ref,
    w2_ref,
    b2_ref,
    wl_ref,
    rate_ref,
    rows_any,
    cols_any,
    twist_any,
    lt_ref,
    c1_ref,
    a2_ref,
    c2_ref,
    raw_ref,
    spec_ref,
    w1_hold,
    w2_hold,
    wl_hold,
    fwd_rows,
    cols,
    twist,
    sems,
):
    step = pl.program_id(0)
    moves = [
        pltpu.make_async_copy(src, dst, sems.at[k])
        for k, (src, dst) in enumerate(
            [(rows_any, fwd_rows), (cols_any, cols), (twist_any, twist)]
        )
    ]

    @pl.when(step == 0)
    def _():
        for move in moves:
            move.start()

        def parts(ref):
            x = ref[...] * (1.0 / math.pi)
            hi = x.astype(BF16).astype(F32)
            return hi, x - hi

        w_hi, w_lo = parts(w1_ref)
        b_hi, b_lo = parts(b1_ref)
        count, hid = w_hi.shape
        gap = jnp.zeros((LO_ROW - ONES_ROW - 2, hid), F32)
        end = jnp.zeros((BLK - HI_ROW - count, hid), F32)
        stack = jnp.concatenate([w_hi, b_hi, b_lo, gap, w_hi, w_lo, end], axis=0)
        w1_hold[...] = stack.T.astype(BF16)
        w_hi, w_lo = parts(w2_ref)
        b_hi, b_lo = parts(b2_ref)
        end = jnp.zeros((14, hid), F32)
        stack = jnp.concatenate([w_hi, w_hi, w_lo, b_hi, b_lo, end], axis=0)
        w2_hold[...] = stack.T.astype(BF16)
        rank = rank_ref[0]
        for h in range(2):
            wl_hold[:, half(h)] = jnp.broadcast_to(
                picked(wl_ref[:, half(h)], rank), (hid, BLK)
            )

    one, cos_one = sin_cos_pi(dot(w1_hold[...], feat_ref[...]))
    c1_ref[...] = cos_one.astype(BF16)
    hi, lo = split(one)
    lt_ref[...] = jnp.concatenate([hi, feat_ref[0:64, :]], axis=0).T
    ones = jnp.ones((16, NET_CHUNK), BF16)
    two, cos_two = sin_cos_pi(dot(w2_hold[...], jnp.concatenate([hi, lo, hi, ones], axis=0)))
    a2_ref[...] = two.astype(BF16)
    c2_ref[...] = cos_two.astype(BF16)
    for h in range(2):
        col = wl_hold[:, h * BLK : h * BLK + 1]
        row = jnp.sum(col * two, axis=0, keepdims=True)
        for j in range(NET_CHUNK // BLK):
            at = step * (NET_CHUNK // BLK) + j
            raw_ref[h, pl.ds(at, 1), :] = row[:, j * BLK : (j + 1) * BLK]

    @pl.when(step == pl.num_programs(0) - 1)
    def _():
        signals = [
            (raw_ref[h] * decay_window(rate_ref, rank_ref[0], h)[0]).astype(BF16)
            for h in range(2)
        ]
        for move in moves:
            move.wait()
        for h, spec in enumerate(forward_spectra(signals, fwd_rows, cols, twist)):
            spec_ref[h] = spec


def owner_kernel(
    rank_ref,
    taps_ref,
    skip_ref,
    rate_ref,
    w2_ref,
    wl_ref,
    recv_ref,
    *refs,
):
    large, back_ref, vec_ref, line_ref, hold_ref = refs[:11], *refs[11:15]
    copies, sems = refs[15:26], refs[26]
    got_ref, got_sem = refs[27:]
    got = pltpu.make_async_copy(recv_ref, got_ref, got_sem)
    got.start()
    fwd_rows, cols, twist, back_cols, back_rows, spec_ref, raw_ref = copies[:7]
    c2_ref, c1_ref, lt_ref, a2_ref = copies[7:]
    moves = [
        pltpu.make_async_copy(src, dst, sems.at[k])
        for k, (src, dst) in enumerate(zip(large, copies))
    ]
    for move in moves[:7]:
        move.start()
    rank = rank_ref[0]
    got.wait()
    for move in moves[7:]:
        move.start()
    hold_ref[...] = got_ref[...].astype(F32)
    taps, gains = [], []
    xs, sides, cots, gated, grad_mixed = [], [], [], [], []
    for h in range(2):
        gains.append(picked(skip_ref[:, half(h)], rank))
        taps.append([])
        for i in range(3):
            own = picked(taps_ref[i, :, half(h)], rank)
            taps[h].append([own[m : m + 1] for m in range(3)])
        x = [hold_ref[:, i * 2 + h, :] for i in range(4)]
        shifted = [[x[i], earlier(x[i], 1), earlier(x[i], 2)] for i in range(3)]
        side = [
            taps[h][i][0] * shifted[i][0]
            + taps[h][i][1] * shifted[i][1]
            + taps[h][i][2] * shifted[i][2]
            for i in range(3)
        ]
        xs.append(shifted)
        sides.append(side)
        cots.append(x[3])
        gated.append((side[1] * side[2]).astype(BF16))
        grad_mixed.append((x[3] * side[0]).astype(BF16))
    for move in moves[:7]:
        move.wait()
    spec = forward_spectra(gated + grad_mixed, fwd_rows, cols, twist)
    pairs = [
        [times(spec[h], spec[2 + h], True) for h in range(2)],
        [times(spec[h], spec_ref[h], False) for h in range(2)],
        [times(spec_ref[h], spec[2 + h], True) for h in range(2)],
    ]
    convs = inverse_pairs(pairs, back_cols, back_rows, twist)

    sums = []
    line_ref[...] = jnp.zeros_like(line_ref)
    for h in range(2):
        grad_filt = convs[h].astype(BF16).astype(F32)
        window, slope = decay_window(rate_ref, rank, h)
        grad_raw = grad_filt * window
        sums.append(jnp.sum(grad_raw * raw_ref[h] * slope, axis=0, keepdims=True))
        for n in range(BLK):
            line_ref[h : h + 1, n * BLK : (n + 1) * BLK] = grad_raw[n : n + 1, :]

    w2_hi, w2_lo = split(w2_ref[...])
    w2_stack = jnp.concatenate([w2_hi, w2_lo], axis=1)
    col0 = picked(wl_ref[:, half(0)], rank)
    col1 = picked(wl_ref[:, half(1)], rank)
    total = jnp.zeros((BLK, BLK), F32)
    last = jnp.zeros((64, 16), F32)
    for move in moves[7:]:
        move.wait()
    for j in range(line_ref.shape[1] // CHUNK):
        at = slice(j * CHUNK, (j + 1) * CHUNK)
        line = line_ref[:, at]
        grad_two = (col0 * line[0:1] + col1 * line[1:2]) * c2_ref[:, at].astype(F32)
        hi = grad_two.astype(BF16)
        grad_one = dot(w2_stack, jnp.concatenate([hi, hi], axis=0)) * c1_ref[
            :, at
        ].astype(F32)
        line_hi = line.astype(BF16).astype(F32)
        lines = jnp.concatenate([line_hi, line - line_hi], axis=0).astype(BF16)
        right = jnp.concatenate([hi, grad_one.astype(BF16)], axis=0)
        total = total + dot(right, lt_ref[at, :])
        last = last + dot_nt(a2_ref[:, at], lines)

    last = jnp.concatenate([last, jnp.zeros((64, BLK - 16), F32)], axis=1).T
    last = last[:8] + last[8:16]
    count = 33
    bias_at = slice(64 + ONES_ROW, 65 + ONES_ROW)
    low = jnp.concatenate(
        [
            total[64:, 64 : 64 + count],
            total[64:, bias_at],
            total[:64, bias_at],
            jnp.zeros((64, 64 - count - 2), F32),
        ],
        axis=1,
    )
    packed = jnp.concatenate([total[:64, :64], low], axis=0)
    p_hi, p_lo = split(packed)
    rows = [None] * 6
    rows[4] = jnp.concatenate([p_hi, p_lo], axis=1)

    lane = places()[1]
    edge = jnp.zeros((BLK, BLK), F32)
    for h in range(2):
        g = gated[h].astype(F32)
        gm = grad_mixed[h].astype(F32)
        mixed = (convs[2 + h] + gains[h] * g).astype(BF16).astype(F32)
        grad_gated = (convs[4 + h] + gains[h] * gm).astype(BF16).astype(F32)
        side = sides[h]
        grad_side = [cots[h] * mixed, grad_gated * side[2], grad_gated * side[1]]
        rows[h] = mixed
        rows[2 + h] = grad_gated
        sums.append(jnp.sum(gm * g, axis=0, keepdims=True))
        for i in range(3):
            at = 2 * (i * 2 + h)
            before = jnp.where(lane < 2, xs[h][i][2], 0.0)
            after = jnp.where(lane >= BLK - 2, later(grad_side[i], 2), 0.0)
            after_hi = after.astype(BF16).astype(F32)
            edge = (
                edge
                + pltpu.roll(before, at, 1)
                + pltpu.roll(after_hi, AHEAD_HI + 2 + at, 1)
                + pltpu.roll(after - after_hi, AHEAD_LO + 2 + at, 1)
            )
            for m in range(3):
                sums.append(jnp.sum(grad_side[i] * xs[h][i][m], axis=0, keepdims=True))
    rows[5] = edge
    for k in range(3):
        pair = [rows[k].astype(F32), rows[3 + k].astype(F32)]
        back_ref[:, :, half(k)] = jnp.stack(pair, axis=1).astype(BF16)
    sums = jnp.concatenate(sums + [jnp.zeros((64 - len(sums), BLK), F32)], axis=0)
    totals = dot_nt(jnp.ones((8, BLK), F32), sums, lax.Precision.HIGHEST)
    vec_ref[...] = jnp.concatenate(
        [jnp.zeros((1, 64), F32), last[0:1], last[1:2], totals[0:1]], axis=1
    )


def rows_kernel(recv_ref, streams_ref, cot_ref, taps_ref, out_ref, grad_ref):
    row = places()[0]
    edge = turned(recv_ref[:, 5 * BLK :])
    for h in range(2):
        mixed = turned(recv_ref[:, half(h)])
        grad_gated = turned(recv_ref[:, half(2 + h)])
        side = []
        for i in range(3):
            at = 2 * (i * 2 + h)
            x = streams_ref[i, :, half(h)].astype(F32)
            far, near = edge[at : at + 1], edge[at + 1 : at + 2]
            one = jnp.where(row == 0, near, pltpu.roll(x, 1, 0))
            two = jnp.where(row == 0, far, jnp.where(row == 1, near, pltpu.roll(x, 2, 0)))
            side.append(
                taps_ref[i, 0:1, half(h)] * x
                + taps_ref[i, 1:2, half(h)] * one
                + taps_ref[i, 2:3, half(h)] * two
            )
        out_ref[:, half(h)] = (side[0] * mixed).astype(BF16)
        cot = cot_ref[:, half(h)].astype(F32)
        grad_side = [cot * mixed, grad_gated * side[2], grad_gated * side[1]]
        for i in range(3):
            at = 2 * (i * 2 + h)
            ahead = (
                edge[AHEAD_HI + at : AHEAD_HI + at + 2] + edge[AHEAD_LO + at : AHEAD_LO + at + 2]
            )
            near, far = ahead[0:1], ahead[1:2]
            g = grad_side[i]
            one = jnp.where(row == BLK - 1, near, pltpu.roll(g, BLK - 1, 0))
            two = jnp.where(
                row == BLK - 1,
                far,
                jnp.where(row == BLK - 2, near, pltpu.roll(g, BLK - 2, 0)),
            )
            grad_ref[i, :, half(h)] = (
                taps_ref[i, 0:1, half(h)] * g
                + taps_ref[i, 1:2, half(h)] * one
                + taps_ref[i, 2:3, half(h)] * two
            ).astype(BF16)


def final_kernel(
    far_ref,
    taps_ref,
    w1_ref,
    b1_ref,
    w2_ref,
    b2_ref,
    wl_ref,
    rate_ref,
    skip_ref,
    all_ref,
    sem,
):
    move = pltpu.make_async_copy(far_ref, all_ref, sem)
    move.start()
    move.wait()
    low = all_ref[:, 0, :BLK].T
    high = all_ref[:, 0, BLK:].T
    shared = low[:64]
    flipped = shared[:, 64:]
    w2_ref[...] = shared[:, :64]
    w1_ref[...] = flipped[:33]
    b1_ref[...] = flipped[33:34]
    b2_ref[...] = flipped[34:35]
    wl_ref[:, :BLK] = low[64:]
    wl_ref[:, BLK:] = high[:64]
    rest = high[64:]
    for h in range(2):
        rate_ref[:, half(h)] = rest[h : h + 1]
        skip_ref[:, half(h)] = rest[2 + 10 * h : 3 + 10 * h]
        for i in range(3):
            at = 3 + 10 * h + 3 * i
            taps_ref[i, :, half(h)] = rest[at : at + 3]


def params(**kwargs):
    return pltpu.CompilerParams(vmem_limit_bytes=VMEM, **kwargs)


def on_device(
    streams,
    short_taps,
    w_first,
    b_first,
    w_second,
    b_second,
    w_last,
    decay_rate,
    skip_gain,
    cotangent,
):
    peers = lax.axis_size("ctx")
    rank = lax.axis_index("ctx")
    tok = streams.shape[1]
    channels = streams.shape[2]
    seq_len = tok * peers
    count, hid = w_first.shape
    vmem = pl.BlockSpec(memory_space=pltpu.VMEM)
    smem = pl.BlockSpec(memory_space=pltpu.SMEM)
    far = pl.BlockSpec(memory_space=pl.ANY)
    shape = jax.ShapeDtypeStruct

    row = rank.reshape(1).astype(jnp.int32)
    outgoing = pl.pallas_call(
        pack_kernel,
        out_shape=shape((peers, 8, tok), BF16),
        scratch_shapes=[pltpu.VMEM((peers, 8, tok), F32)],
        name="pack_rows",
    )(streams, cotangent)
    incoming = lax.all_to_all(outgoing, "ctx", split_axis=0, concat_axis=0, tiled=True)

    fwd_rows, cols, twist, back_cols, back_rows = (jnp.asarray(c) for c in dft_consts())
    feat = jnp.asarray(feature_const(seq_len, (count - 1) // 2))
    act = shape((hid, seq_len), BF16)
    act_spec = pl.BlockSpec((hid, NET_CHUNK), lambda j: (0, j))
    whole = lambda *dims: pl.BlockSpec(dims, lambda j: (0,) * len(dims))
    lt, c1, a2, c2, raw, filt_spec = pl.pallas_call(
        net_kernel,
        grid=(seq_len // NET_CHUNK,),
        in_specs=[
            smem,
            pl.BlockSpec((BLK, NET_CHUNK), lambda j: (0, j)),
            whole(count, hid),
            whole(1, hid),
            whole(hid, hid),
            whole(1, hid),
            whole(hid, channels),
            whole(1, channels),
            far,
            far,
            far,
        ],
        out_specs=[
            pl.BlockSpec((NET_CHUNK, BLK), lambda j: (j, 0)),
            act_spec,
            act_spec,
            act_spec,
            whole(2, BLK, BLK),
            whole(2, SIDE, SIDE),
        ],
        out_shape=[shape((seq_len, BLK), BF16), act, act, act, shape((2, BLK, BLK), F32), shape((2, SIDE, SIDE), F32)],
        scratch_shapes=[
            pltpu.VMEM((hid, BLK), BF16),
            pltpu.VMEM((hid, 3 * hid + 16), BF16),
            pltpu.VMEM((hid, 2 * BLK), F32),
            pltpu.VMEM(fwd_rows.shape, BF16),
            pltpu.VMEM(cols.shape, BF16),
            pltpu.VMEM(twist.shape, F32),
            pltpu.SemaphoreType.DMA((3,)),
        ],
        compiler_params=params(dimension_semantics=("arbitrary",)),
        name="filter_net",
    )(
        row,
        feat,
        w_first,
        b_first[None],
        w_second,
        b_second[None],
        w_last,
        decay_rate[None],
        fwd_rows,
        cols,
        twist,
    )

    large = [fwd_rows, cols, twist, back_cols, back_rows, filt_spec, raw, c2, c1, lt, a2]
    back, vec = pl.pallas_call(
        owner_kernel,
        in_specs=[smem] + [vmem] * 5 + [far] * 12,
        out_specs=[vmem, vmem],
        out_shape=[shape((peers, 2, 3 * tok), BF16), shape((1, 2 * BLK), F32)],
        scratch_shapes=[
            pltpu.VMEM((8, seq_len), F32),
            pltpu.VMEM((peers, 8, tok), F32),
            *[pltpu.VMEM(x.shape, x.dtype) for x in large],
            pltpu.SemaphoreType.DMA((len(large),)),
            pltpu.VMEM((peers, 8, tok), BF16),
            pltpu.SemaphoreType.DMA,
        ],
        compiler_params=params(),
        name="convolve_channels",
    )(
        row,
        short_taps,
        skip_gain[None],
        decay_rate[None],
        w_second,
        w_last,
        incoming,
        *large,
    )
    returned = lax.all_to_all(back, "ctx", split_axis=0, concat_axis=0, tiled=True)
    returned, vec = lax.optimization_barrier((returned, vec))
    halves = jnp.sum(returned[:, 1, tok : 2 * tok].astype(F32), axis=0)
    returned = returned.reshape(peers, 6 * tok)
    mine = lax.psum(halves[:64] + halves[64:], "tp")
    vec = jnp.concatenate([mine[None], vec[:, 64:]], axis=1)
    spread = jnp.broadcast_to(vec[None], (peers, 1, 2 * BLK))
    gathered = lax.all_to_all(spread, "ctx", split_axis=0, concat_axis=0, tiled=True)
    output, grad_streams = pl.pallas_call(
        rows_kernel,
        out_shape=[shape((tok, channels), BF16), shape((3, tok, channels), BF16)],
        compiler_params=params(),
        name="finish_rows",
    )(returned, streams, cotangent, short_taps)
    taps, gw1, gb1, gw2, gb2, gwl, rate, skip = pl.pallas_call(
        final_kernel,
        in_specs=[far],
        scratch_shapes=[pltpu.VMEM((peers, 1, 2 * BLK), F32), pltpu.SemaphoreType.DMA],
        out_shape=[
            shape((3, 3, channels), F32),
            shape((count, hid), F32),
            shape((1, hid), F32),
            shape((hid, hid), F32),
            shape((1, hid), F32),
            shape((hid, channels), F32),
            shape((1, channels), F32),
            shape((1, channels), F32),
        ],
        name="unpack_sums",
    )(gathered)
    return (
        output,
        grad_streams,
        taps,
        gw1,
        gb1[0],
        gw2,
        gb2[0],
        gwl,
        rate[0],
        skip[0],
    )


def solution(mesh):
    return jax.shard_map(
        on_device,
        mesh=mesh,
        in_specs=(
            P(None, "ctx", "tp"),
            P(None, None, "tp"),
            P(),
            P(),
            P(),
            P(),
            P(None, "tp"),
            P("tp"),
            P("tp"),
            P("ctx", "tp"),
        ),
        out_specs=(
            P("ctx", "tp"),
            P(None, "ctx", "tp"),
            P(None, None, "tp"),
            P(),
            P(),
            P(),
            P(),
            P(None, "tp"),
            P("tp"),
            P("tp"),
        ),
        check_vma=False,
    )
```
